32 devices in a mesh: pipe: 2 (over core), seq: 4 (over z), chan: 4 (over y, x).
Axes of the slice: x: 2, y: 2, z: 4, core: 2. Of those that a mesh axis runs over, the one named last changes fastest.
Arguments:
- grad_out: bfloat16 [2, 1024, 2048], P('pipe', 'seq', 'chan'), may hold values from -6 to 6
- value_branch: bfloat16 [2, 1024, 2048], P('pipe', 'seq', 'chan'), may hold values from -0.1875 to 0.1875
- key_gate: bfloat16 [2, 1024, 2048], P('pipe', 'seq', 'chan'), may hold values from -6 to 6
- query_gate: bfloat16 [2, 1024, 2048], P('pipe', 'seq', 'chan'), may hold values from -6 to 6
- short_weights: float32 [2, 3, 2048], P('pipe', None, 'chan'), may hold values from -3 to 3
- long_filters: bfloat16 [2, 1024, 2048], P('pipe', 'seq', 'chan'), may hold values from -0.1875 to 0.1875
Outputs:
- passed_grad: bfloat16 [2, 1024, 2048], P('pipe', 'seq', 'chan')
- filter_grad: float32 [2, 1024, 2048], P('pipe', 'seq', 'chan')
The draws below stay inside these ranges and needn't reach their ends.
All inputs are finite; a program needn't handle non-finite values.
Results may differ from the reference program's by a relative error of at most 0.0049.
Values may be sent and summed in bfloat16 or wider, within the bound.
A program may use at most 64 MiB of HBM per device.

```python
import jax
import jax.numpy as jnp
from jax import lax

CHANNELS = 2048
TOKENS = 1024
SECTIONS = 2


def steps_of(own_key, extent, pieces, smallest, top_value):
    gain = 1.0
    for axis_at, blocks in pieces:
        draws = jax.random.uniform(jax.random.fold_in(jax.random.fold_in(own_key, 6), axis_at), (blocks,), jnp.float32, smallest / len(pieces), top_value / len(pieces))
        gain = gain * jnp.repeat(jnp.exp(draws), extent[axis_at] // blocks).reshape((-1,) + (1,) * (len(extent) - 1 - axis_at))
    return gain


def normal_values(key, dims, spread, reach, shards=(), held_as=jnp.bfloat16):
    entries = jax.random.normal(key, dims, jnp.float32) * spread
    if len(shards) > 0:
        entries = steps_of(key, dims, shards, -0.22, 0.18) * entries
    return jnp.clip(entries, min=-reach, max=reach).astype(held_as)


def setup_inputs(seed: int = 0) -> dict:
    key_of = jax.random.split(jax.random.key(seed), 7)
    return {
        "grad_out": normal_values(key_of[0], (SECTIONS, TOKENS, CHANNELS), 1.0, 6.0, ((0, 2), (1, 4), (2, 4))),
        "value_branch": normal_values(key_of[1], (SECTIONS, TOKENS, CHANNELS), TOKENS ** -0.5, 0.1875, ((0, 2), (1, 4), (2, 4))),
        "key_gate": normal_values(key_of[2], (SECTIONS, TOKENS, CHANNELS), 1.0, 6.0, ((0, 2), (1, 4), (2, 4))),
        "query_gate": normal_values(key_of[3], (SECTIONS, TOKENS, CHANNELS), 1.0, 6.0, ((0, 2), (1, 4), (2, 4))),
        "short_weights": normal_values(key_of[4], (SECTIONS, 3, CHANNELS), 0.5, 3.0, ((0, 2), (2, 4)), jnp.float32),
        "long_filters": normal_values(key_of[5], (SECTIONS, TOKENS, CHANNELS), TOKENS ** -0.5, 0.1875, ((0, 2), (1, 4), (2, 4))),
    }


def one_section(grad_y, value_in, key_in, query_in, weights, filter_in):
    length = grad_y.shape[0]
    padded = 2 * length
    grad_conv = lax.optimization_barrier((query_in.astype(jnp.float32) * grad_y.astype(jnp.float32)).astype(jnp.bfloat16)).astype(jnp.float32)
    gated_value = lax.optimization_barrier((key_in.astype(jnp.float32) * value_in.astype(jnp.float32)).astype(jnp.bfloat16)).astype(jnp.float32)
    spec_conv = jnp.fft.rfft(grad_conv, n=padded, axis=0)
    spec_filter = jnp.fft.rfft(filter_in.astype(jnp.float32), n=padded, axis=0)
    grad_gated = jnp.fft.irfft(spec_conv * jnp.conj(spec_filter), n=padded, axis=0)[:length]
    spec_gated = jnp.fft.rfft(gated_value, n=padded, axis=0)
    filter_grad = jnp.fft.irfft(spec_conv * jnp.conj(spec_gated), n=padded, axis=0)[:length]
    grad_value = key_in.astype(jnp.float32) * grad_gated
    longer = jnp.concatenate([grad_value, jnp.zeros((2, CHANNELS), grad_value.dtype)], axis=0)
    grad_input = weights[0] * longer[:length] + weights[1] * longer[1:length + 1] + weights[2] * longer[2:]
    return grad_input.astype(jnp.bfloat16), filter_grad


def reference(grad_out, value_branch, key_gate, query_gate, short_weights, long_filters):
    inputs_list = []
    filters_list = []
    for section in range(SECTIONS):
        grad_input, filter_grad = one_section(grad_out[section], value_branch[section], key_gate[section], query_gate[section], short_weights[section], long_filters[section])
        inputs_list.append(grad_input)
        filters_list.append(filter_grad)
    passed_grad = jnp.stack([inputs_list[(section + 1) % SECTIONS] for section in range(SECTIONS)])
    return passed_grad, jnp.stack(filters_list)
```

```python
import functools
import math

import jax
import jax.numpy as jnp
import numpy as np
from jax import lax
from jax.experimental import pallas as pl
from jax.experimental.pallas import tpu as pltpu
from jax.sharding import PartitionSpec as P


def from_behind(value, axis, by):
    devices = lax.axis_size(axis)
    pairs = [(i, i + by) for i in range(devices) if 0 <= i + by < devices]
    return lax.ppermute(value, axis, pairs)


def shifted(block, axis, distance):
    devices = range(lax.axis_size(axis))
    route = [((i - distance) % len(devices), i) for i in devices]
    return lax.ppermute(block, axis, route)


def phase_table(product, modulus):
    angles = (product % modulus).astype(jnp.float32) * (2.0 * math.pi / modulus)
    return (jnp.cos(angles), jnp.sin(angles))


def contract(form, table, values):
    return jnp.einsum(form, table, values, precision=lax.Precision.HIGHEST)


def forward_blocks(signal, row_first, padded):
    block_count = signal.shape[0]
    row_count = signal.shape[1]
    frequency = jnp.arange(2 * block_count, dtype=jnp.int32)
    block_index = jnp.arange(block_count, dtype=jnp.int32)
    cos_table, sin_table = phase_table(frequency[:, None] * block_index[None, :], 2 * block_count)
    real_part = contract("ca,arx->crx", cos_table, signal)
    imag_part = -contract("ca,arx->crx", sin_table, signal)
    row_index = row_first + jnp.arange(row_count, dtype=jnp.int32)
    cos_twist, sin_twist = phase_table(frequency[:, None] * row_index[None, :], padded)
    cos_twist = cos_twist[:, :, None]
    sin_twist = sin_twist[:, :, None]
    return (
        real_part * cos_twist + imag_part * sin_twist,
        imag_part * cos_twist - real_part * sin_twist,
    )


def along_rows(real_part, imag_part, direction):
    length = real_part.shape[1]
    indices = jnp.arange(length, dtype=jnp.int32)
    cos_table, sin_table = phase_table(indices[:, None] * indices[None, :], length)
    cos_real = contract("dr,crx->cdx", cos_table, real_part)
    cos_imag = contract("dr,crx->cdx", cos_table, imag_part)
    sin_real = contract("dr,crx->cdx", sin_table, real_part)
    sin_imag = contract("dr,crx->cdx", sin_table, imag_part)
    return (cos_real - direction * sin_imag, cos_imag + direction * sin_real)


def inverse_twist(real_part, imag_part, freq_first, padded):
    frequency = freq_first + jnp.arange(real_part.shape[0], dtype=jnp.int32)
    row_index = jnp.arange(real_part.shape[1], dtype=jnp.int32)
    cos_twist, sin_twist = phase_table(frequency[:, None] * row_index[None, :], padded)
    cos_twist = cos_twist[:, :, None]
    sin_twist = sin_twist[:, :, None]
    return (
        real_part * cos_twist - imag_part * sin_twist,
        imag_part * cos_twist + real_part * sin_twist,
    )


def inverse_blocks(real_part, imag_part, padded):
    block_count = real_part.shape[0] // 2
    block_index = jnp.arange(block_count, dtype=jnp.int32)
    frequency = jnp.arange(2 * block_count, dtype=jnp.int32)
    cos_table, sin_table = phase_table(block_index[:, None] * frequency[None, :], 2 * block_count)
    summed = contract("ac,crx->arx", cos_table, real_part) - contract(
        "ac,crx->arx", sin_table, imag_part
    )
    return summed * (1.0 / padded)


def spectral_products(conv_real, conv_imag, gated_real, gated_imag, filter_real, filter_imag):
    back_real = conv_real * filter_real + conv_imag * filter_imag
    back_imag = conv_imag * filter_real - conv_real * filter_imag
    fold_real = conv_real * gated_real + conv_imag * gated_imag
    fold_imag = conv_imag * gated_real - conv_real * gated_imag
    return (back_real, back_imag, fold_real, fold_imag)


def spread_body(grad_out, value_branch, key_gate, query_gate, short_weights, long_filters):
    grad_y = grad_out[0]
    tok_rows, columns = grad_y.shape
    devices = lax.axis_size("seq")
    position = lax.axis_index("seq")
    padded = 2 * tok_rows * devices
    key_values = key_gate[0].astype(jnp.float32)
    grad_conv = (query_gate[0].astype(jnp.float32) * grad_y.astype(jnp.float32)).astype(
        jnp.bfloat16
    )
    gated_value = (key_values * value_branch[0].astype(jnp.float32)).astype(jnp.bfloat16)
    per_device = tok_rows // devices
    pieces = (
        lax.all_to_all(grad_conv[None], "seq", split_axis=1, concat_axis=0, tiled=True),
        lax.all_to_all(gated_value[None], "seq", split_axis=1, concat_axis=0, tiled=True),
        lax.all_to_all(long_filters, "seq", split_axis=1, concat_axis=0, tiled=True),
    )
    halves = [
        forward_blocks(piece.astype(jnp.float32), position * per_device, padded) for piece in pieces
    ]
    exchanged = (
        lax.all_to_all(halves[0][0], "seq", split_axis=0, concat_axis=1, tiled=True),
        lax.all_to_all(halves[0][1], "seq", split_axis=0, concat_axis=1, tiled=True),
        lax.all_to_all(halves[1][0], "seq", split_axis=0, concat_axis=1, tiled=True),
        lax.all_to_all(halves[1][1], "seq", split_axis=0, concat_axis=1, tiled=True),
        lax.all_to_all(halves[2][0], "seq", split_axis=0, concat_axis=1, tiled=True),
        lax.all_to_all(halves[2][1], "seq", split_axis=0, concat_axis=1, tiled=True),
    )
    conv_real, conv_imag = along_rows(exchanged[0], exchanged[1], -1.0)
    gated_real, gated_imag = along_rows(exchanged[2], exchanged[3], -1.0)
    filter_real, filter_imag = along_rows(exchanged[4], exchanged[5], -1.0)
    back_real, back_imag, fold_real, fold_imag = spectral_products(
        conv_real, conv_imag, gated_real, gated_imag, filter_real, filter_imag
    )
    pair_count = fold_real.shape[0]
    back_real, back_imag = along_rows(back_real, back_imag, 1.0)
    back_real, back_imag = inverse_twist(back_real, back_imag, position * pair_count, padded)
    fold_real, fold_imag = along_rows(fold_real, fold_imag, 1.0)
    fold_real, fold_imag = inverse_twist(fold_real, fold_imag, position * pair_count, padded)
    returned = (
        lax.all_to_all(back_real, "seq", split_axis=1, concat_axis=0, tiled=True),
        lax.all_to_all(back_imag, "seq", split_axis=1, concat_axis=0, tiled=True),
        lax.all_to_all(fold_real, "seq", split_axis=1, concat_axis=0, tiled=True),
        lax.all_to_all(fold_imag, "seq", split_axis=1, concat_axis=0, tiled=True),
    )
    settled = (
        lax.all_to_all(
            inverse_blocks(returned[0], returned[1], padded),
            "seq",
            split_axis=0,
            concat_axis=1,
            tiled=True,
        ),
        lax.all_to_all(
            inverse_blocks(returned[2], returned[3], padded),
            "seq",
            split_axis=0,
            concat_axis=1,
            tiled=True,
        ),
    )
    grad_gated = settled[0][0]
    grad_filter = settled[1][0]
    grad_value = key_values * grad_gated
    next_rim = from_behind(grad_value[:2], "seq", -1)
    longer = jnp.concatenate([grad_value, next_rim], axis=0)
    weights = short_weights[0]
    grad_input = (
        weights[0] * longer[:tok_rows]
        + weights[1] * longer[1 : tok_rows + 1]
        + weights[2] * longer[2:]
    )
    passed = shifted(grad_input.astype(jnp.bfloat16)[None], "pipe", -1)
    return (passed, grad_filter[None])


LANES = 128
RIM = 16
MESH = pl.DeviceIdType.MESH


def half_step_tables(tokens):
    odd = 2 * np.arange(tokens, dtype=np.int64)[:, None] + 1
    turns = (odd * np.arange(tokens, dtype=np.int64)[None, :]) % (4 * tokens)
    angles = turns * (2.0 * np.pi / (4 * tokens))
    forward = np.concatenate([np.cos(angles), np.sin(angles)], axis=0)
    pairs = []
    for table in (forward, forward.T):
        high = table.astype(jnp.bfloat16)
        low = (table - high.astype(np.float64)).astype(jnp.bfloat16)
        pairs += [high, low]
    return pairs


def relay_kernel(
    devices, go, vb, kg, qg, sw, lf, fwd_hi_hbm, fwd_lo_hbm, inv_hi_hbm, inv_lo_hbm,
    passed, fold_out,
    conv_src, gated_src, conv_all, filt_all, gated_all, fwd_hi, fwd_lo, inv_hi, inv_lo,
    spec_conv, spec_other, packed, back_src, fold_src, back_got, fold_got, key_got, weight_got,
    table_sem, own_sem, send_sem, recv_sem, back_send, back_recv, side_send, side_recv,
):
    rows = go.shape[1]
    tokens = rows * devices
    pipe = lax.axis_index("pipe")
    me = lax.axis_index("seq")
    other = 1 - pipe

    tables = [
        pltpu.make_async_copy(source, target, table_sem.at[i])
        for i, (source, target) in enumerate(
            ((fwd_hi_hbm, fwd_hi), (fwd_lo_hbm, fwd_lo), (inv_hi_hbm, inv_hi), (inv_lo_hbm, inv_lo))
        )
    ]

    def peer(distance):
        return lax.rem(me + distance, devices)

    barrier = pltpu.get_barrier_semaphore()
    for distance in range(devices):
        if distance:
            pl.semaphore_signal(
                barrier, inc=1, device_id={"pipe": pipe, "seq": peer(distance)}, device_id_type=MESH
            )
        pl.semaphore_signal(
            barrier, inc=1, device_id={"pipe": other, "seq": peer(distance)}, device_id_type=MESH
        )
    for copy in tables:
        copy.start()
    conv_src[...] = (qg[0].astype(jnp.float32) * go[0].astype(jnp.float32)).astype(jnp.bfloat16)
    gated_src[...] = (kg[0].astype(jnp.float32) * vb[0].astype(jnp.float32)).astype(jnp.bfloat16)
    back_src[pl.ds(tokens, RIM), :] = jnp.zeros((RIM, LANES), jnp.bfloat16)
    pl.semaphore_wait(barrier, 2 * devices - 1)

    def lanes_of(device):
        return pl.ds(pl.multiple_of(device * LANES, LANES), LANES)

    def rows_of(device, extra=0):
        return pl.ds(pl.multiple_of(device * rows, rows), rows + extra)

    def scatter(kind, source, target):
        own = pltpu.make_async_copy(
            source.at[:, lanes_of(me)], target.at[rows_of(me)], own_sem.at[kind]
        )
        own.start()
        copies = []
        for distance in range(1, devices):
            copy = pltpu.make_async_remote_copy(
                src_ref=source.at[:, lanes_of(peer(distance))],
                dst_ref=target.at[rows_of(me)],
                send_sem=send_sem.at[kind, distance],
                recv_sem=recv_sem.at[kind, distance],
                device_id={"pipe": pipe, "seq": peer(distance)},
                device_id_type=MESH,
            )
            copy.start()
            copies.append(copy)
        return own, copies

    def landed(group):
        own, copies = group
        own.wait()
        for copy in copies:
            copy.wait_recv()

    filt_group = scatter(0, lf.at[0], filt_all)
    conv_group = scatter(1, conv_src, conv_all)
    gated_group = scatter(2, gated_src, gated_all)
    side = []
    for i, (source, target, at) in enumerate(
        (
            (kg.at[0], key_got.at[pl.ds(0, rows)], me),
            (kg.at[0, pl.ds(0, RIM)], key_got.at[pl.ds(rows, RIM)], peer(devices - 1)),
            (sw.at[0], weight_got, me),
        )
    ):
        copy = pltpu.make_async_remote_copy(
            src_ref=source, dst_ref=target, send_sem=side_send.at[i], recv_sem=side_recv.at[i],
            device_id={"pipe": other, "seq": at}, device_id_type=MESH,
        )
        copy.start()
        side.append(copy)

    step = tokens // 2

    def transform(signal, target):
        @pl.loop(0, 2 * tokens // step)
        def _(part):
            at = pl.ds(pl.multiple_of(part * step, step), step)
            values = signal[...]
            target[at, :] = jnp.dot(
                fwd_hi[at, :], values, preferred_element_type=jnp.float32
            ) + jnp.dot(fwd_lo[at, :], values, preferred_element_type=jnp.float32)

    def pack(at, value):
        high = value.astype(jnp.bfloat16)
        packed[at, pl.ds(0, LANES)] = high
        packed[at, pl.ds(LANES, LANES)] = (value - high.astype(jnp.float32)).astype(jnp.bfloat16)

    def correlate(target):
        chunk = rows

        @pl.loop(0, tokens // chunk)
        def _(part):
            top = pl.ds(pl.multiple_of(part * chunk, chunk), chunk)
            low = pl.ds(pl.multiple_of(tokens + part * chunk, chunk), chunk)
            conv_cos, conv_sin = spec_conv[top, :], spec_conv[low, :]
            other_cos, other_sin = spec_other[top, :], spec_other[low, :]
            scale = 1.0 / tokens
            pack(top, (conv_cos * other_cos + conv_sin * other_sin) * scale)
            pack(low, (conv_sin * other_cos - conv_cos * other_sin) * scale)

        @pl.loop(0, tokens // chunk)
        def _(part):
            at = pl.ds(pl.multiple_of(part * chunk, chunk), chunk)
            wide = jnp.dot(inv_hi[at, :], packed[...], preferred_element_type=jnp.float32)
            narrow = jnp.dot(
                inv_lo[at, :], packed[:, pl.ds(0, LANES)], preferred_element_type=jnp.float32
            )
            target[at, :] = (wide[:, :LANES] + wide[:, LANES:] + narrow).astype(jnp.bfloat16)

    landed(filt_group)
    tables[0].wait()
    tables[1].wait()
    transform(filt_all, spec_other)
    landed(conv_group)
    transform(conv_all, spec_conv)
    tables[2].wait()
    tables[3].wait()
    correlate(back_src)
    backs = []
    for distance in range(devices):
        copy = pltpu.make_async_remote_copy(
            src_ref=back_src.at[rows_of(peer(distance), RIM)],
            dst_ref=back_got.at[me],
            send_sem=back_send.at[distance],
            recv_sem=back_recv.at[distance],
            device_id={"pipe": other, "seq": peer(distance)},
            device_id_type=MESH,
        )
        copy.start()
        backs.append(copy)

    landed(gated_group)
    transform(gated_all, spec_other)
    correlate(fold_src)
    own = pltpu.make_async_copy(fold_src.at[rows_of(me)], fold_got.at[me], own_sem.at[3])
    own.start()
    folds = []
    for distance in range(1, devices):
        copy = pltpu.make_async_remote_copy(
            src_ref=fold_src.at[rows_of(peer(distance))],
            dst_ref=fold_got.at[me],
            send_sem=send_sem.at[3, distance],
            recv_sem=recv_sem.at[3, distance],
            device_id={"pipe": pipe, "seq": peer(distance)},
            device_id_type=MESH,
        )
        copy.start()
        folds.append(copy)

    for copy in side + backs:
        copy.wait_recv()
    for block in range(devices):
        columns = pl.ds(block * LANES, LANES)
        value = key_got[:, columns].astype(jnp.float32) * back_got[block].astype(jnp.float32)
        extent = rows + RIM
        total = weight_got[pl.ds(0, 1), columns] * value
        total += weight_got[pl.ds(1, 1), columns] * pltpu.roll(value, extent - 1, 0)
        total += weight_got[pl.ds(2, 1), columns] * pltpu.roll(value, extent - 2, 0)
        passed[0, :, columns] = total[:rows].astype(jnp.bfloat16)
    own.wait()
    for copy in folds:
        copy.wait_recv()
    for block in range(devices):
        fold_out[0, :, pl.ds(block * LANES, LANES)] = fold_got[block].astype(jnp.float32)
    for copy in filt_group[1] + conv_group[1] + gated_group[1] + side + backs + folds:
        copy.wait_send()


def relay_body(grad_out, value_branch, key_gate, query_gate, short_weights, long_filters):
    _, rows, columns = grad_out.shape
    devices = lax.axis_size("seq")
    tokens = rows * devices
    tables = [jnp.asarray(table) for table in half_step_tables(tokens)]
    vmem = pl.BlockSpec(memory_space=pltpu.VMEM)
    anywhere = pl.BlockSpec(memory_space=pl.ANY)
    half, full = jnp.bfloat16, jnp.float32
    return pl.pallas_call(
        functools.partial(relay_kernel, devices),
        out_shape=(
            jax.ShapeDtypeStruct((1, rows, columns), half),
            jax.ShapeDtypeStruct((1, rows, columns), full),
        ),
        in_specs=[vmem] * 6 + [anywhere] * 4,
        out_specs=(vmem, vmem),
        scratch_shapes=[
            pltpu.VMEM((rows, columns), half),
            pltpu.VMEM((rows, columns), half),
            pltpu.VMEM((tokens, LANES), half),
            pltpu.VMEM((tokens, LANES), half),
            pltpu.VMEM((tokens, LANES), half),
            pltpu.VMEM((2 * tokens, tokens), half),
            pltpu.VMEM((2 * tokens, tokens), half),
            pltpu.VMEM((tokens, 2 * tokens), half),
            pltpu.VMEM((tokens, 2 * tokens), half),
            pltpu.VMEM((2 * tokens, LANES), full),
            pltpu.VMEM((2 * tokens, LANES), full),
            pltpu.VMEM((2 * tokens, 2 * LANES), half),
            pltpu.VMEM((tokens + RIM, LANES), half),
            pltpu.VMEM((tokens, LANES), half),
            pltpu.VMEM((devices, rows + RIM, LANES), half),
            pltpu.VMEM((devices, rows, LANES), half),
            pltpu.VMEM((rows + RIM, columns), half),
            pltpu.VMEM((3, columns), full),
            pltpu.SemaphoreType.DMA((4,)),
            pltpu.SemaphoreType.DMA((4,)),
            pltpu.SemaphoreType.DMA((4, devices)),
            pltpu.SemaphoreType.DMA((4, devices)),
            pltpu.SemaphoreType.DMA((devices,)),
            pltpu.SemaphoreType.DMA((devices,)),
            pltpu.SemaphoreType.DMA((3,)),
            pltpu.SemaphoreType.DMA((3,)),
        ],
        compiler_params=pltpu.CompilerParams(
            collective_id=0, has_side_effects=True, vmem_limit_bytes=44 * 2**20
        ),
        cost_estimate=pl.CostEstimate(
            flops=28 * tokens * tokens * LANES, bytes_accessed=16 * tokens * tokens, transcendentals=0
        ),
    )(grad_out, value_branch, key_gate, query_gate, short_weights, long_filters, *tables)


def solution(mesh):
    placed = (
        P("pipe", "seq", "chan"),
        P("pipe", "seq", "chan"),
        P("pipe", "seq", "chan"),
        P("pipe", "seq", "chan"),
        P("pipe", None, "chan"),
        P("pipe", "seq", "chan"),
    )

    def run(*arrays):
        _, tokens, channels = arrays[0].shape
        devices = mesh.shape["seq"]
        fits = (
            mesh.shape["pipe"] == 2
            and devices > 1
            and channels == mesh.shape["chan"] * devices * LANES
            and tokens <= 1024
            and tokens % (devices * RIM) == 0
        )
        return jax.shard_map(
            relay_body if fits else spread_body,
            mesh=mesh,
            in_specs=placed,
            out_specs=(P("pipe", "seq", "chan"), P("pipe", "seq", "chan")),
            check_vma=False,
        )(*arrays)

    return run
```

```python
import functools
import math

import jax
import jax.numpy as jnp
import numpy as np
from jax import lax
from jax.experimental import pallas as pl
from jax.experimental.pallas import tpu as pltpu
from jax.sharding import PartitionSpec as P


def from_behind(value, axis, by):
    devices = lax.axis_size(axis)
    pairs = [(i, i + by) for i in range(devices) if 0 <= i + by < devices]
    return lax.ppermute(value, axis, pairs)


def shifted(block, axis, distance):
    devices = range(lax.axis_size(axis))
    route = [((i - distance) % len(devices), i) for i in devices]
    return lax.ppermute(block, axis, route)


def phase_table(product, modulus):
    angles = (product % modulus).astype(jnp.float32) * (2.0 * math.pi / modulus)
    return (jnp.cos(angles), jnp.sin(angles))


def contract(form, table, values):
    return jnp.einsum(form, table, values, precision=lax.Precision.HIGHEST)


def forward_blocks(signal, row_first, padded):
    block_count = signal.shape[0]
    row_count = signal.shape[1]
    frequency = jnp.arange(2 * block_count, dtype=jnp.int32)
    block_index = jnp.arange(block_count, dtype=jnp.int32)
    cos_table, sin_table = phase_table(frequency[:, None] * block_index[None, :], 2 * block_count)
    real_part = contract("ca,arx->crx", cos_table, signal)
    imag_part = -contract("ca,arx->crx", sin_table, signal)
    row_index = row_first + jnp.arange(row_count, dtype=jnp.int32)
    cos_twist, sin_twist = phase_table(frequency[:, None] * row_index[None, :], padded)
    cos_twist = cos_twist[:, :, None]
    sin_twist = sin_twist[:, :, None]
    return (
        real_part * cos_twist + imag_part * sin_twist,
        imag_part * cos_twist - real_part * sin_twist,
    )


def along_rows(real_part, imag_part, direction):
    length = real_part.shape[1]
    indices = jnp.arange(length, dtype=jnp.int32)
    cos_table, sin_table = phase_table(indices[:, None] * indices[None, :], length)
    cos_real = contract("dr,crx->cdx", cos_table, real_part)
    cos_imag = contract("dr,crx->cdx", cos_table, imag_part)
    sin_real = contract("dr,crx->cdx", sin_table, real_part)
    sin_imag = contract("dr,crx->cdx", sin_table, imag_part)
    return (cos_real - direction * sin_imag, cos_imag + direction * sin_real)


def inverse_twist(real_part, imag_part, freq_first, padded):
    frequency = freq_first + jnp.arange(real_part.shape[0], dtype=jnp.int32)
    row_index = jnp.arange(real_part.shape[1], dtype=jnp.int32)
    cos_twist, sin_twist = phase_table(frequency[:, None] * row_index[None, :], padded)
    cos_twist = cos_twist[:, :, None]
    sin_twist = sin_twist[:, :, None]
    return (
        real_part * cos_twist - imag_part * sin_twist,
        imag_part * cos_twist + real_part * sin_twist,
    )


def inverse_blocks(real_part, imag_part, padded):
    block_count = real_part.shape[0] // 2
    block_index = jnp.arange(block_count, dtype=jnp.int32)
    frequency = jnp.arange(2 * block_count, dtype=jnp.int32)
    cos_table, sin_table = phase_table(block_index[:, None] * frequency[None, :], 2 * block_count)
    summed = contract("ac,crx->arx", cos_table, real_part) - contract(
        "ac,crx->arx", sin_table, imag_part
    )
    return summed * (1.0 / padded)


def spectral_products(conv_real, conv_imag, gated_real, gated_imag, filter_real, filter_imag):
    back_real = conv_real * filter_real + conv_imag * filter_imag
    back_imag = conv_imag * filter_real - conv_real * filter_imag
    fold_real = conv_real * gated_real + conv_imag * gated_imag
    fold_imag = conv_imag * gated_real - conv_real * gated_imag
    return (back_real, back_imag, fold_real, fold_imag)


def spread_body(grad_out, value_branch, key_gate, query_gate, short_weights, long_filters):
    grad_y = grad_out[0]
    tok_rows, columns = grad_y.shape
    devices = lax.axis_size("seq")
    position = lax.axis_index("seq")
    padded = 2 * tok_rows * devices
    key_values = key_gate[0].astype(jnp.float32)
    grad_conv = (query_gate[0].astype(jnp.float32) * grad_y.astype(jnp.float32)).astype(
        jnp.bfloat16
    )
    gated_value = (key_values * value_branch[0].astype(jnp.float32)).astype(jnp.bfloat16)
    per_device = tok_rows // devices
    pieces = (
        lax.all_to_all(grad_conv[None], "seq", split_axis=1, concat_axis=0, tiled=True),
        lax.all_to_all(gated_value[None], "seq", split_axis=1, concat_axis=0, tiled=True),
        lax.all_to_all(long_filters, "seq", split_axis=1, concat_axis=0, tiled=True),
    )
    halves = [
        forward_blocks(piece.astype(jnp.float32), position * per_device, padded) for piece in pieces
    ]
    exchanged = (
        lax.all_to_all(halves[0][0], "seq", split_axis=0, concat_axis=1, tiled=True),
        lax.all_to_all(halves[0][1], "seq", split_axis=0, concat_axis=1, tiled=True),
        lax.all_to_all(halves[1][0], "seq", split_axis=0, concat_axis=1, tiled=True),
        lax.all_to_all(halves[1][1], "seq", split_axis=0, concat_axis=1, tiled=True),
        lax.all_to_all(halves[2][0], "seq", split_axis=0, concat_axis=1, tiled=True),
        lax.all_to_all(halves[2][1], "seq", split_axis=0, concat_axis=1, tiled=True),
    )
    conv_real, conv_imag = along_rows(exchanged[0], exchanged[1], -1.0)
    gated_real, gated_imag = along_rows(exchanged[2], exchanged[3], -1.0)
    filter_real, filter_imag = along_rows(exchanged[4], exchanged[5], -1.0)
    back_real, back_imag, fold_real, fold_imag = spectral_products(
        conv_real, conv_imag, gated_real, gated_imag, filter_real, filter_imag
    )
    pair_count = fold_real.shape[0]
    back_real, back_imag = along_rows(back_real, back_imag, 1.0)
    back_real, back_imag = inverse_twist(back_real, back_imag, position * pair_count, padded)
    fold_real, fold_imag = along_rows(fold_real, fold_imag, 1.0)
    fold_real, fold_imag = inverse_twist(fold_real, fold_imag, position * pair_count, padded)
    returned = (
        lax.all_to_all(back_real, "seq", split_axis=1, concat_axis=0, tiled=True),
        lax.all_to_all(back_imag, "seq", split_axis=1, concat_axis=0, tiled=True),
        lax.all_to_all(fold_real, "seq", split_axis=1, concat_axis=0, tiled=True),
        lax.all_to_all(fold_imag, "seq", split_axis=1, concat_axis=0, tiled=True),
    )
    settled = (
        lax.all_to_all(
            inverse_blocks(returned[0], returned[1], padded),
            "seq",
            split_axis=0,
            concat_axis=1,
            tiled=True,
        ),
        lax.all_to_all(
            inverse_blocks(returned[2], returned[3], padded),
            "seq",
            split_axis=0,
            concat_axis=1,
            tiled=True,
        ),
    )
    grad_gated = settled[0][0]
    grad_filter = settled[1][0]
    grad_value = key_values * grad_gated
    next_rim = from_behind(grad_value[:2], "seq", -1)
    longer = jnp.concatenate([grad_value, next_rim], axis=0)
    weights = short_weights[0]
    grad_input = (
        weights[0] * longer[:tok_rows]
        + weights[1] * longer[1 : tok_rows + 1]
        + weights[2] * longer[2:]
    )
    passed = shifted(grad_input.astype(jnp.bfloat16)[None], "pipe", -1)
    return (passed, grad_filter[None])


LANES = 128
RIM = 16
PARTS = 2
MESH = pl.DeviceIdType.MESH


def half_step_tables(tokens, devices):
    half = tokens // 2
    odd = 2 * np.arange(half, dtype=np.int64)[:, None] + 1
    turns = (odd * np.arange(tokens, dtype=np.int64)[None, :]) % (4 * tokens)
    angles = turns * (2.0 * np.pi / (4 * tokens))
    part = half // PARTS
    share = tokens // devices // 2
    forward, inverse = [], []
    for parity in range(2):
        cosines, sines = np.cos(angles[:, parity::2]), np.sin(angles[:, parity::2])
        for first in range(0, half, part):
            forward.append(pair(np.concatenate([cosines[first : first + part], sines[first : first + part]])))
        back = np.concatenate([cosines, sines]).T
        back = np.concatenate([back, np.zeros((RIM, 2 * half))])
        for first in range(0, half, share):
            inverse.append(pair(back[first : first + share + RIM]))
    return (
        np.stack(forward).reshape(2, PARTS, 4 * part, half),
        np.stack(inverse).reshape(2, devices, 2 * (share + RIM), 2 * half),
    )


def pair(table):
    high = table.astype(jnp.bfloat16)
    low = (table - high.astype(np.float64)).astype(jnp.bfloat16)
    return np.concatenate([high, low])


def relay_kernel(
    devices, go_hbm, vb_hbm, kg_hbm, qg_hbm, sw, lf, fwd_hbm, inv_hbm,
    passed, fold_out,
    go, vb, kg, qg,
    conv_src, gated_src, conv_all, filt_all, gated_all, fwd, inv, mixed,
    spec_conv, spec_other, packed, back_src, fold_src, back_got, fold_got, key_got, weight_got,
    load_sem, own_sem, send_sem, recv_sem, back_send, back_recv, side_send, side_recv,
):
    rows = go.shape[0]
    tokens = rows * devices
    half = tokens // 2
    share = rows // 2
    pipe = lax.axis_index("pipe")
    me = lax.axis_index("seq")
    other = 1 - pipe
    far_first = sorted(range(1, devices), key=lambda d: (abs(2 * d - devices), d))

    loads = []
    for i, (source, target) in enumerate(
        ((go_hbm.at[0], go), (qg_hbm.at[0], qg), (kg_hbm.at[0], kg), (vb_hbm.at[0], vb), (fwd_hbm, fwd), (inv_hbm, inv))
    ):
        copy = pltpu.make_async_copy(source, target, load_sem.at[i])
        copy.start()
        loads.append(copy)

    def peer(distance):
        return lax.rem(me + distance, devices)

    def behind(distance):
        return lax.rem(me + devices - distance, devices)

    barrier = pltpu.get_barrier_semaphore()
    for distance in range(devices):
        if distance:
            pl.semaphore_signal(
                barrier, inc=1, device_id={"pipe": pipe, "seq": peer(distance)}, device_id_type=MESH
            )
        pl.semaphore_signal(
            barrier, inc=1, device_id={"pipe": other, "seq": peer(distance)}, device_id_type=MESH
        )
    loads[0].wait()
    loads[1].wait()
    conv_src[...] = (qg[...].astype(jnp.float32) * go[...].astype(jnp.float32)).astype(jnp.bfloat16)
    pl.semaphore_wait(barrier, 2 * devices - 1)

    def lanes_of(device):
        return pl.ds(pl.multiple_of(device * LANES, LANES), LANES)

    def rows_of(device):
        return pl.ds(pl.multiple_of(device * rows, rows), rows)

    def scatter(kind, source, target):
        copies = []
        for distance in far_first:
            copy = pltpu.make_async_remote_copy(
                src_ref=source.at[:, lanes_of(peer(distance))],
                dst_ref=target.at[rows_of(me)],
                send_sem=send_sem.at[kind, distance],
                recv_sem=recv_sem.at[kind, distance],
                device_id={"pipe": pipe, "seq": peer(distance)},
                device_id_type=MESH,
            )
            copy.start()
            copies.append(copy)
        own = pltpu.make_async_copy(
            source.at[:, lanes_of(me)], target.at[rows_of(me)], own_sem.at[kind]
        )
        own.start()
        return own, copies

    def landed(group):
        own, copies = group
        own.wait()
        for copy in copies:
            copy.wait_recv()

    filt_group = scatter(0, lf.at[0], filt_all)
    conv_group = scatter(1, conv_src, conv_all)
    loads[2].wait()
    loads[3].wait()
    gated_src[...] = (kg[...].astype(jnp.float32) * vb[...].astype(jnp.float32)).astype(jnp.bfloat16)
    gated_group = scatter(2, gated_src, gated_all)
    side = []
    for i, (source, target, at) in enumerate(
        (
            (kg, key_got.at[pl.ds(0, rows)], me),
            (kg.at[pl.ds(0, RIM)], key_got.at[pl.ds(rows, RIM)], behind(1)),
            (sw, weight_got, me),
        )
    ):
        copy = pltpu.make_async_remote_copy(
            src_ref=source, dst_ref=target, send_sem=side_send.at[i], recv_sem=side_recv.at[i],
            device_id={"pipe": other, "seq": at}, device_id_type=MESH,
        )
        copy.start()
        side.append(copy)

    part = half // PARTS

    def transform(signal, target):
        mixed[pl.ds(0, tokens), :] = signal[...].astype(jnp.float32)
        evens = mixed[pl.ds(0, half, stride=2), :].astype(jnp.bfloat16)
        odds = mixed[pl.ds(1, half, stride=2), :].astype(jnp.bfloat16)
        for i in range(PARTS):
            even = jnp.dot(fwd[0, i], evens, preferred_element_type=jnp.float32)
            even = even[: 2 * part] + even[2 * part :]
            odd = jnp.dot(fwd[1, i], odds, preferred_element_type=jnp.float32)
            odd = odd[: 2 * part] + odd[2 * part :]
            at = pl.ds(i * part, part)
            target[0, at, :] = even[:part] + odd[:part]
            target[1, at, :] = even[:part] - odd[:part]
            target[2, at, :] = odd[part:] + even[part:]
            target[3, at, :] = odd[part:] - even[part:]

    def pack(parity, at, value):
        high = value.astype(jnp.bfloat16)
        packed[parity, at, pl.ds(0, LANES)] = high
        packed[parity, at, pl.ds(LANES, LANES)] = (value - high.astype(jnp.float32)).astype(jnp.bfloat16)

    def multiply():
        chunk = LANES

        @pl.loop(0, half // chunk)
        def _(step):
            at = pl.ds(pl.multiple_of(step * chunk, chunk), chunk)
            low = pl.ds(pl.multiple_of(half + step * chunk, chunk), chunk)
            scale = 1.0 / tokens
            alike, cross = [], []
            for side_at in range(2):
                conv_cos, conv_sin = spec_conv[side_at, at, :] * scale, spec_conv[2 + side_at, at, :] * scale
                other_cos, other_sin = spec_other[side_at, at, :], spec_other[2 + side_at, at, :]
                alike.append(conv_cos * other_cos + conv_sin * other_sin)
                cross.append(conv_sin * other_cos - conv_cos * other_sin)
            pack(0, at, alike[0] + alike[1])
            pack(0, low, cross[0] - cross[1])
            pack(1, at, alike[0] - alike[1])
            pack(1, low, cross[0] + cross[1])

    def invert(block):
        for parity in range(2):
            wide = jnp.dot(inv[parity, block], packed[parity], preferred_element_type=jnp.float32)
            wide = wide[: share + RIM] + wide[share + RIM :]
            wide = wide[:, :LANES] + wide[:, LANES:]
            mixed[pl.ds(parity, share + RIM, stride=2), :] = wide

    landed(filt_group)
    loads[4].wait()
    transform(filt_all, spec_other)
    landed(conv_group)
    transform(conv_all, spec_conv)
    multiply()
    loads[5].wait()
    backs = []
    for distance in far_first + [0]:
        invert(peer(distance))
        back_src[distance] = mixed[pl.ds(0, rows + RIM), :].astype(jnp.bfloat16)
        copy = pltpu.make_async_remote_copy(
            src_ref=back_src.at[distance],
            dst_ref=back_got.at[me],
            send_sem=back_send.at[distance],
            recv_sem=back_recv.at[distance],
            device_id={"pipe": other, "seq": peer(distance)},
            device_id_type=MESH,
        )
        copy.start()
        backs.append(copy)

    landed(gated_group)
    transform(gated_all, spec_other)
    multiply()
    folds = []
    for distance in far_first:
        invert(peer(distance))
        fold_src[distance] = mixed[pl.ds(0, rows), :].astype(jnp.bfloat16)
        copy = pltpu.make_async_remote_copy(
            src_ref=fold_src.at[distance],
            dst_ref=fold_got.at[me],
            send_sem=send_sem.at[3, distance],
            recv_sem=recv_sem.at[3, distance],
            device_id={"pipe": pipe, "seq": peer(distance)},
            device_id_type=MESH,
        )
        copy.start()
        folds.append(copy)
    invert(me)
    fold_out[0, :, lanes_of(me)] = mixed[pl.ds(0, rows), :]

    for copy in side:
        copy.wait_recv()
    for copy, distance in zip(backs, far_first + [0]):
        copy.wait_recv()
        columns = lanes_of(behind(distance))
        value = key_got[:, columns].astype(jnp.float32) * back_got[behind(distance)].astype(jnp.float32)
        extent = rows + RIM
        total = weight_got[0, :, columns] * value
        total += weight_got[1, :, columns] * pltpu.roll(value, extent - 1, 0)
        total += weight_got[2, :, columns] * pltpu.roll(value, extent - 2, 0)
        passed[0, :, columns] = total[:rows].astype(jnp.bfloat16)
    for copy, distance in zip(folds, far_first):
        copy.wait_recv()
        fold_out[0, :, lanes_of(behind(distance))] = fold_got[behind(distance)].astype(jnp.float32)
    for copy in filt_group[1] + conv_group[1] + gated_group[1] + side + backs + folds:
        copy.wait_send()


def relay_body(grad_out, value_branch, key_gate, query_gate, short_weights, long_filters):
    _, rows, columns = grad_out.shape
    devices = lax.axis_size("seq")
    tokens = rows * devices
    tables = [jnp.asarray(table) for table in half_step_tables(tokens, devices)]
    vmem = pl.BlockSpec(memory_space=pltpu.VMEM)
    anywhere = pl.BlockSpec(memory_space=pltpu.HBM)
    half, full = jnp.bfloat16, jnp.float32
    return pl.pallas_call(
        functools.partial(relay_kernel, devices),
        out_shape=(
            jax.ShapeDtypeStruct((1, rows, columns), half),
            jax.ShapeDtypeStruct((1, rows, columns), full),
        ),
        in_specs=[anywhere] * 8,
        out_specs=(vmem, vmem),
        scratch_shapes=[pltpu.VMEM((rows, columns), half)] * 6
        + [pltpu.VMEM((tokens, LANES), half)] * 3
        + [
            pltpu.VMEM(tables[0].shape, half),
            pltpu.VMEM(tables[1].shape, half),
            pltpu.VMEM((tokens + 2 * RIM, LANES), full),
            pltpu.VMEM((4, tokens // 2, LANES), full),
            pltpu.VMEM((4, tokens // 2, LANES), full),
            pltpu.VMEM((2, tokens, 2 * LANES), half),
            pltpu.VMEM((devices, rows + RIM, LANES), half),
            pltpu.VMEM((devices, rows, LANES), half),
            pltpu.VMEM((devices, rows + RIM, LANES), half),
            pltpu.VMEM((devices, rows, LANES), half),
            pltpu.VMEM((rows + RIM, columns), half),
            pltpu.VMEM((3, 1, columns), full),
            pltpu.SemaphoreType.DMA((6,)),
            pltpu.SemaphoreType.DMA((3,)),
            pltpu.SemaphoreType.DMA((4, devices)),
            pltpu.SemaphoreType.DMA((4, devices)),
            pltpu.SemaphoreType.DMA((devices,)),
            pltpu.SemaphoreType.DMA((devices,)),
            pltpu.SemaphoreType.DMA((3,)),
            pltpu.SemaphoreType.DMA((3,)),
        ],
        compiler_params=pltpu.CompilerParams(
            collective_id=0, has_side_effects=True, vmem_limit_bytes=63 * 2**20
        ),
        cost_estimate=pl.CostEstimate(
            flops=16 * tokens * tokens * LANES, bytes_accessed=10 * tokens * tokens, transcendentals=0
        ),
    )(
        grad_out, value_branch, key_gate, query_gate,
        jnp.transpose(short_weights, (1, 0, 2)), long_filters, *tables,
    )


def solution(mesh):
    placed = (
        P("pipe", "seq", "chan"),
        P("pipe", "seq", "chan"),
        P("pipe", "seq", "chan"),
        P("pipe", "seq", "chan"),
        P("pipe", None, "chan"),
        P("pipe", "seq", "chan"),
    )

    def run(*arrays):
        _, tokens, channels = arrays[0].shape
        devices = mesh.shape["seq"]
        fits = (
            mesh.shape["pipe"] == 2
            and devices > 1
            and channels == mesh.shape["chan"] * devices * LANES
            and tokens <= 1024
            and tokens % (2 * devices * RIM) == 0
            and tokens % (2 * LANES) == 0
        )
        return jax.shard_map(
            relay_body if fits else spread_body,
            mesh=mesh,
            in_specs=placed,
            out_specs=(P("pipe", "seq", "chan"), P("pipe", "seq", "chan")),
            check_vma=False,
        )(*arrays)

    return run
```

```python
import functools
import math

import jax
import jax.numpy as jnp
import numpy as np
from jax import lax
from jax.experimental import pallas as pl
from jax.experimental.pallas import tpu as pltpu
from jax.sharding import PartitionSpec as P


def from_behind(value, axis, by):
    devices = lax.axis_size(axis)
    pairs = [(i, i + by) for i in range(devices) if 0 <= i + by < devices]
    return lax.ppermute(value, axis, pairs)


def shifted(block, axis, distance):
    devices = range(lax.axis_size(axis))
    route = [((i - distance) % len(devices), i) for i in devices]
    return lax.ppermute(block, axis, route)


def phase_table(product, modulus):
    angles = (product % modulus).astype(jnp.float32) * (2.0 * math.pi / modulus)
    return (jnp.cos(angles), jnp.sin(angles))


def contract(form, table, values):
    return jnp.einsum(form, table, values, precision=lax.Precision.HIGHEST)


def forward_blocks(signal, row_first, padded):
    block_count = signal.shape[0]
    row_count = signal.shape[1]
    frequency = jnp.arange(2 * block_count, dtype=jnp.int32)
    block_index = jnp.arange(block_count, dtype=jnp.int32)
    cos_table, sin_table = phase_table(frequency[:, None] * block_index[None, :], 2 * block_count)
    real_part = contract("ca,arx->crx", cos_table, signal)
    imag_part = -contract("ca,arx->crx", sin_table, signal)
    row_index = row_first + jnp.arange(row_count, dtype=jnp.int32)
    cos_twist, sin_twist = phase_table(frequency[:, None] * row_index[None, :], padded)
    cos_twist = cos_twist[:, :, None]
    sin_twist = sin_twist[:, :, None]
    return (
        real_part * cos_twist + imag_part * sin_twist,
        imag_part * cos_twist - real_part * sin_twist,
    )


def along_rows(real_part, imag_part, direction):
    length = real_part.shape[1]
    indices = jnp.arange(length, dtype=jnp.int32)
    cos_table, sin_table = phase_table(indices[:, None] * indices[None, :], length)
    cos_real = contract("dr,crx->cdx", cos_table, real_part)
    cos_imag = contract("dr,crx->cdx", cos_table, imag_part)
    sin_real = contract("dr,crx->cdx", sin_table, real_part)
    sin_imag = contract("dr,crx->cdx", sin_table, imag_part)
    return (cos_real - direction * sin_imag, cos_imag + direction * sin_real)


def inverse_twist(real_part, imag_part, freq_first, padded):
    frequency = freq_first + jnp.arange(real_part.shape[0], dtype=jnp.int32)
    row_index = jnp.arange(real_part.shape[1], dtype=jnp.int32)
    cos_twist, sin_twist = phase_table(frequency[:, None] * row_index[None, :], padded)
    cos_twist = cos_twist[:, :, None]
    sin_twist = sin_twist[:, :, None]
    return (
        real_part * cos_twist - imag_part * sin_twist,
        imag_part * cos_twist + real_part * sin_twist,
    )


def inverse_blocks(real_part, imag_part, padded):
    block_count = real_part.shape[0] // 2
    block_index = jnp.arange(block_count, dtype=jnp.int32)
    frequency = jnp.arange(2 * block_count, dtype=jnp.int32)
    cos_table, sin_table = phase_table(block_index[:, None] * frequency[None, :], 2 * block_count)
    summed = contract("ac,crx->arx", cos_table, real_part) - contract(
        "ac,crx->arx", sin_table, imag_part
    )
    return summed * (1.0 / padded)


def spectral_products(conv_real, conv_imag, gated_real, gated_imag, filter_real, filter_imag):
    back_real = conv_real * filter_real + conv_imag * filter_imag
    back_imag = conv_imag * filter_real - conv_real * filter_imag
    fold_real = conv_real * gated_real + conv_imag * gated_imag
    fold_imag = conv_imag * gated_real - conv_real * gated_imag
    return (back_real, back_imag, fold_real, fold_imag)


def spread_body(grad_out, value_branch, key_gate, query_gate, short_weights, long_filters):
    grad_y = grad_out[0]
    tok_rows, columns = grad_y.shape
    devices = lax.axis_size("seq")
    position = lax.axis_index("seq")
    padded = 2 * tok_rows * devices
    key_values = key_gate[0].astype(jnp.float32)
    grad_conv = (query_gate[0].astype(jnp.float32) * grad_y.astype(jnp.float32)).astype(
        jnp.bfloat16
    )
    gated_value = (key_values * value_branch[0].astype(jnp.float32)).astype(jnp.bfloat16)
    per_device = tok_rows // devices
    pieces = (
        lax.all_to_all(grad_conv[None], "seq", split_axis=1, concat_axis=0, tiled=True),
        lax.all_to_all(gated_value[None], "seq", split_axis=1, concat_axis=0, tiled=True),
        lax.all_to_all(long_filters, "seq", split_axis=1, concat_axis=0, tiled=True),
    )
    halves = [
        forward_blocks(piece.astype(jnp.float32), position * per_device, padded) for piece in pieces
    ]
    exchanged = (
        lax.all_to_all(halves[0][0], "seq", split_axis=0, concat_axis=1, tiled=True),
        lax.all_to_all(halves[0][1], "seq", split_axis=0, concat_axis=1, tiled=True),
        lax.all_to_all(halves[1][0], "seq", split_axis=0, concat_axis=1, tiled=True),
        lax.all_to_all(halves[1][1], "seq", split_axis=0, concat_axis=1, tiled=True),
        lax.all_to_all(halves[2][0], "seq", split_axis=0, concat_axis=1, tiled=True),
        lax.all_to_all(halves[2][1], "seq", split_axis=0, concat_axis=1, tiled=True),
    )
    conv_real, conv_imag = along_rows(exchanged[0], exchanged[1], -1.0)
    gated_real, gated_imag = along_rows(exchanged[2], exchanged[3], -1.0)
    filter_real, filter_imag = along_rows(exchanged[4], exchanged[5], -1.0)
    back_real, back_imag, fold_real, fold_imag = spectral_products(
        conv_real, conv_imag, gated_real, gated_imag, filter_real, filter_imag
    )
    pair_count = fold_real.shape[0]
    back_real, back_imag = along_rows(back_real, back_imag, 1.0)
    back_real, back_imag = inverse_twist(back_real, back_imag, position * pair_count, padded)
    fold_real, fold_imag = along_rows(fold_real, fold_imag, 1.0)
    fold_real, fold_imag = inverse_twist(fold_real, fold_imag, position * pair_count, padded)
    returned = (
        lax.all_to_all(back_real, "seq", split_axis=1, concat_axis=0, tiled=True),
        lax.all_to_all(back_imag, "seq", split_axis=1, concat_axis=0, tiled=True),
        lax.all_to_all(fold_real, "seq", split_axis=1, concat_axis=0, tiled=True),
        lax.all_to_all(fold_imag, "seq", split_axis=1, concat_axis=0, tiled=True),
    )
    settled = (
        lax.all_to_all(
            inverse_blocks(returned[0], returned[1], padded),
            "seq",
            split_axis=0,
            concat_axis=1,
            tiled=True,
        ),
        lax.all_to_all(
            inverse_blocks(returned[2], returned[3], padded),
            "seq",
            split_axis=0,
            concat_axis=1,
            tiled=True,
        ),
    )
    grad_gated = settled[0][0]
    grad_filter = settled[1][0]
    grad_value = key_values * grad_gated
    next_rim = from_behind(grad_value[:2], "seq", -1)
    longer = jnp.concatenate([grad_value, next_rim], axis=0)
    weights = short_weights[0]
    grad_input = (
        weights[0] * longer[:tok_rows]
        + weights[1] * longer[1 : tok_rows + 1]
        + weights[2] * longer[2:]
    )
    passed = shifted(grad_input.astype(jnp.bfloat16)[None], "pipe", -1)
    return (passed, grad_filter[None])


LANES = 128
RIM = 16
PARTS = 2
MESH = pl.DeviceIdType.MESH


def half_step_tables(tokens, devices):
    half = tokens // 2
    odd = 2 * np.arange(half, dtype=np.int64)[:, None] + 1
    turns = (odd * np.arange(tokens, dtype=np.int64)[None, :]) % (4 * tokens)
    angles = turns * (2.0 * np.pi / (4 * tokens))
    part = half // PARTS
    share = tokens // devices // 2
    forward, inverse = [], []
    for parity in range(2):
        cosines, sines = np.cos(angles[:, parity::2]), np.sin(angles[:, parity::2])
        for first in range(0, half, part):
            forward.append(pair(np.concatenate([cosines[first : first + part], sines[first : first + part]])))
        back = np.concatenate([cosines, sines]).T
        back = np.concatenate([back, np.zeros((RIM, 2 * half))])
        for first in range(0, half, share):
            inverse.append(pair(back[first : first + share + RIM]))
    return (
        np.stack(forward).reshape(2, PARTS, 4 * part, half),
        np.stack(inverse).reshape(2, devices, 2 * (share + RIM), 2 * half),
    )


def pair(table):
    high = table.astype(jnp.bfloat16)
    low = (table - high.astype(np.float64)).astype(jnp.bfloat16)
    return np.concatenate([high, low])


def relay_kernel(
    devices, go_hbm, vb_hbm, kg_hbm, qg_hbm, sw, lf, fwd_hbm, inv_hbm,
    passed, fold_out,
    go, vb, kg, qg,
    conv_src, gated_src, filt_src, conv_all, filt_all, gated_all, fwd, inv, mixed,
    spec_conv, spec_other, packed, back_src, fold_src, back_got, fold_got, key_got, weight_got,
    load_sem, filt_sem, own_sem, send_sem, recv_sem, back_send, back_recv, side_send, side_recv,
):
    rows = go.shape[0]
    tokens = rows * devices
    half = tokens // 2
    share = rows // 2
    pipe = lax.axis_index("pipe")
    me = lax.axis_index("seq")
    other = 1 - pipe
    far_first = sorted(range(1, devices), key=lambda d: (abs(2 * d - devices), d))

    loads = []
    for i, (source, target) in enumerate(
        ((go_hbm.at[0], go), (qg_hbm.at[0], qg), (kg_hbm.at[0], kg), (vb_hbm.at[0], vb), (fwd_hbm, fwd), (inv_hbm, inv))
    ):
        copy = pltpu.make_async_copy(source, target, load_sem.at[i])
        copy.start()
        loads.append(copy)

    filt_loads = []
    for block in range(devices):
        copy = pltpu.make_async_copy(
            lf.at[0, :, pl.ds(block * LANES, LANES)], filt_src.at[block], filt_sem.at[block]
        )
        copy.start()
        filt_loads.append(copy)

    def gate(left, right, target):
        for block in range(devices):
            columns = pl.ds(block * LANES, LANES)
            value = left[:, columns].astype(jnp.float32) * right[:, columns].astype(jnp.float32)
            target[block] = value.astype(jnp.bfloat16)

    def peer(distance):
        return lax.rem(me + distance, devices)

    def behind(distance):
        return lax.rem(me + devices - distance, devices)

    barrier = pltpu.get_barrier_semaphore()
    for distance in range(devices):
        if distance:
            pl.semaphore_signal(
                barrier, inc=1, device_id={"pipe": pipe, "seq": peer(distance)}, device_id_type=MESH
            )
        pl.semaphore_signal(
            barrier, inc=1, device_id={"pipe": other, "seq": peer(distance)}, device_id_type=MESH
        )
    loads[0].wait()
    loads[1].wait()
    gate(qg, go, conv_src)
    for copy in filt_loads:
        copy.wait()
    pl.semaphore_wait(barrier, 2 * devices - 1)

    def lanes_of(device):
        return pl.ds(pl.multiple_of(device * LANES, LANES), LANES)

    def rows_of(device):
        return pl.ds(pl.multiple_of(device * rows, rows), rows)

    def scatter(kind, source, target):
        copies = []
        for distance in far_first:
            copy = pltpu.make_async_remote_copy(
                src_ref=source.at[peer(distance)],
                dst_ref=target.at[rows_of(me)],
                send_sem=send_sem.at[kind, distance],
                recv_sem=recv_sem.at[kind, distance],
                device_id={"pipe": pipe, "seq": peer(distance)},
                device_id_type=MESH,
            )
            copy.start()
            copies.append(copy)
        own = pltpu.make_async_copy(
            source.at[me], target.at[rows_of(me)], own_sem.at[kind]
        )
        own.start()
        return own, copies

    def landed(group):
        own, copies = group
        own.wait()
        for copy in copies:
            copy.wait_recv()

    filt_group = scatter(0, filt_src, filt_all)
    conv_group = scatter(1, conv_src, conv_all)
    loads[2].wait()
    loads[3].wait()
    gate(kg, vb, gated_src)
    side = []
    for i, (source, target, at) in enumerate(
        (
            (kg, key_got.at[pl.ds(0, rows)], me),
            (kg.at[pl.ds(0, RIM)], key_got.at[pl.ds(rows, RIM)], behind(1)),
            (sw, weight_got, me),
        )
    ):
        copy = pltpu.make_async_remote_copy(
            src_ref=source, dst_ref=target, send_sem=side_send.at[i], recv_sem=side_recv.at[i],
            device_id={"pipe": other, "seq": at}, device_id_type=MESH,
        )
        copy.start()
        side.append(copy)

    for copy in filt_group[1]:
        copy.wait_send()
    gated_group = scatter(2, gated_src, gated_all)
    part = half // PARTS

    def transform(signal, target):
        mixed[pl.ds(0, tokens), :] = signal[...].astype(jnp.float32)
        evens = mixed[pl.ds(0, half, stride=2), :].astype(jnp.bfloat16)
        odds = mixed[pl.ds(1, half, stride=2), :].astype(jnp.bfloat16)
        for i in range(PARTS):
            even = jnp.dot(fwd[0, i], evens, preferred_element_type=jnp.float32)
            even = even[: 2 * part] + even[2 * part :]
            odd = jnp.dot(fwd[1, i], odds, preferred_element_type=jnp.float32)
            odd = odd[: 2 * part] + odd[2 * part :]
            at = pl.ds(i * part, part)
            target[0, at, :] = even[:part] + odd[:part]
            target[1, at, :] = even[:part] - odd[:part]
            target[2, at, :] = odd[part:] + even[part:]
            target[3, at, :] = odd[part:] - even[part:]

    def pack(parity, at, value):
        high = value.astype(jnp.bfloat16)
        packed[parity, at, pl.ds(0, LANES)] = high
        packed[parity, at, pl.ds(LANES, LANES)] = (value - high.astype(jnp.float32)).astype(jnp.bfloat16)

    def multiply():
        chunk = LANES

        @pl.loop(0, half // chunk)
        def _(step):
            at = pl.ds(pl.multiple_of(step * chunk, chunk), chunk)
            low = pl.ds(pl.multiple_of(half + step * chunk, chunk), chunk)
            scale = 1.0 / tokens
            alike, cross = [], []
            for side_at in range(2):
                conv_cos, conv_sin = spec_conv[side_at, at, :] * scale, spec_conv[2 + side_at, at, :] * scale
                other_cos, other_sin = spec_other[side_at, at, :], spec_other[2 + side_at, at, :]
                alike.append(conv_cos * other_cos + conv_sin * other_sin)
                cross.append(conv_sin * other_cos - conv_cos * other_sin)
            pack(0, at, alike[0] + alike[1])
            pack(0, low, cross[0] - cross[1])
            pack(1, at, alike[0] - alike[1])
            pack(1, low, cross[0] + cross[1])

    def invert(block):
        for parity in range(2):
            wide = jnp.dot(inv[parity, block], packed[parity], preferred_element_type=jnp.float32)
            wide = wide[: share + RIM] + wide[share + RIM :]
            wide = wide[:, :LANES] + wide[:, LANES:]
            mixed[pl.ds(parity, share + RIM, stride=2), :] = wide

    landed(filt_group)
    loads[4].wait()
    transform(filt_all, spec_other)
    landed(conv_group)
    transform(conv_all, spec_conv)
    multiply()
    loads[5].wait()
    backs = []
    for distance in far_first + [0]:
        invert(peer(distance))
        back_src[distance] = mixed[pl.ds(0, rows + RIM), :].astype(jnp.bfloat16)
        copy = pltpu.make_async_remote_copy(
            src_ref=back_src.at[distance],
            dst_ref=back_got.at[me],
            send_sem=back_send.at[distance],
            recv_sem=back_recv.at[distance],
            device_id={"pipe": other, "seq": peer(distance)},
            device_id_type=MESH,
        )
        copy.start()
        backs.append(copy)

    landed(gated_group)
    transform(gated_all, spec_other)
    multiply()
    folds = []
    for distance in far_first:
        invert(peer(distance))
        fold_src[distance] = mixed[pl.ds(0, rows), :].astype(jnp.bfloat16)
        copy = pltpu.make_async_remote_copy(
            src_ref=fold_src.at[distance],
            dst_ref=fold_got.at[me],
            send_sem=send_sem.at[3, distance],
            recv_sem=recv_sem.at[3, distance],
            device_id={"pipe": pipe, "seq": peer(distance)},
            device_id_type=MESH,
        )
        copy.start()
        folds.append(copy)
    invert(me)
    fold_out[0, :, lanes_of(me)] = mixed[pl.ds(0, rows), :]

    for copy in side:
        copy.wait_recv()
    for copy, distance in zip(backs, far_first + [0]):
        copy.wait_recv()
        columns = lanes_of(behind(distance))
        value = key_got[:, columns].astype(jnp.float32) * back_got[behind(distance)].astype(jnp.float32)
        extent = rows + RIM
        total = weight_got[0, :, columns] * value
        total += weight_got[1, :, columns] * pltpu.roll(value, extent - 1, 0)
        total += weight_got[2, :, columns] * pltpu.roll(value, extent - 2, 0)
        passed[0, :, columns] = total[:rows].astype(jnp.bfloat16)
    for copy, distance in zip(folds, far_first):
        copy.wait_recv()
        fold_out[0, :, lanes_of(behind(distance))] = fold_got[behind(distance)].astype(jnp.float32)
    for copy in conv_group[1] + gated_group[1] + side + backs + folds:
        copy.wait_send()


def relay_body(grad_out, value_branch, key_gate, query_gate, short_weights, long_filters):
    _, rows, columns = grad_out.shape
    devices = lax.axis_size("seq")
    tokens = rows * devices
    tables = [jnp.asarray(table) for table in half_step_tables(tokens, devices)]
    vmem = pl.BlockSpec(memory_space=pltpu.VMEM)
    anywhere = pl.BlockSpec(memory_space=pltpu.HBM)
    half, full = jnp.bfloat16, jnp.float32
    return pl.pallas_call(
        functools.partial(relay_kernel, devices),
        out_shape=(
            pltpu.VMEM((1, rows, columns), half),
            pltpu.VMEM((1, rows, columns), full),
        ),
        in_specs=[anywhere] * 8,
        out_specs=(vmem, vmem),
        scratch_shapes=[pltpu.VMEM((rows, columns), half)] * 4
        + [pltpu.VMEM((devices, rows, LANES), half)] * 3
        + [pltpu.VMEM((tokens, LANES), half)] * 3
        + [
            pltpu.VMEM(tables[0].shape, half),
            pltpu.VMEM(tables[1].shape, half),
            pltpu.VMEM((tokens + 2 * RIM, LANES), full),
            pltpu.VMEM((4, tokens // 2, LANES), full),
            pltpu.VMEM((4, tokens // 2, LANES), full),
            pltpu.VMEM((2, tokens, 2 * LANES), half),
            pltpu.VMEM((devices, rows + RIM, LANES), half),
            pltpu.VMEM((devices, rows, LANES), half),
            pltpu.VMEM((devices, rows + RIM, LANES), half),
            pltpu.VMEM((devices, rows, LANES), half),
            pltpu.VMEM((rows + RIM, columns), half),
            pltpu.VMEM((3, 1, columns), full),
            pltpu.SemaphoreType.DMA((6,)),
            pltpu.SemaphoreType.DMA((devices,)),
            pltpu.SemaphoreType.DMA((3,)),
            pltpu.SemaphoreType.DMA((4, devices)),
            pltpu.SemaphoreType.DMA((4, devices)),
            pltpu.SemaphoreType.DMA((devices,)),
            pltpu.SemaphoreType.DMA((devices,)),
            pltpu.SemaphoreType.DMA((3,)),
            pltpu.SemaphoreType.DMA((3,)),
        ],
        compiler_params=pltpu.CompilerParams(
            collective_id=0, has_side_effects=True, vmem_limit_bytes=62 * 2**20
        ),
        cost_estimate=pl.CostEstimate(
            flops=16 * tokens * tokens * LANES, bytes_accessed=10 * tokens * tokens, transcendentals=0
        ),
    )(
        grad_out, value_branch, key_gate, query_gate,
        jnp.transpose(short_weights, (1, 0, 2)), long_filters, *tables,
    )


def solution(mesh):
    placed = (
        P("pipe", "seq", "chan"),
        P("pipe", "seq", "chan"),
        P("pipe", "seq", "chan"),
        P("pipe", "seq", "chan"),
        P("pipe", None, "chan"),
        P("pipe", "seq", "chan"),
    )

    def run(*arrays):
        _, tokens, channels = arrays[0].shape
        devices = mesh.shape["seq"]
        fits = (
            mesh.shape["pipe"] == 2
            and devices > 1
            and channels == mesh.shape["chan"] * devices * LANES
            and tokens <= 1024
            and tokens % (2 * devices * RIM) == 0
            and tokens % (2 * LANES) == 0
        )
        return jax.shard_map(
            relay_body if fits else spread_body,
            mesh=mesh,
            in_specs=placed,
            out_specs=(P("pipe", "seq", "chan"), P("pipe", "seq", "chan")),
            check_vma=False,
        )(*arrays)

    return run
```

```python
import functools
import math

import jax
import jax.numpy as jnp
import numpy as np
from jax import lax
from jax.experimental import pallas as pl
from jax.experimental.pallas import tpu as pltpu
from jax.sharding import PartitionSpec as P


def from_behind(value, axis, by):
    devices = lax.axis_size(axis)
    pairs = [(i, i + by) for i in range(devices) if 0 <= i + by < devices]
    return lax.ppermute(value, axis, pairs)


def shifted(block, axis, distance):
    devices = range(lax.axis_size(axis))
    route = [((i - distance) % len(devices), i) for i in devices]
    return lax.ppermute(block, axis, route)


def phase_table(product, modulus):
    angles = (product % modulus).astype(jnp.float32) * (2.0 * math.pi / modulus)
    return (jnp.cos(angles), jnp.sin(angles))


def contract(form, table, values):
    return jnp.einsum(form, table, values, precision=lax.Precision.HIGHEST)


def forward_blocks(signal, row_first, padded):
    block_count = signal.shape[0]
    row_count = signal.shape[1]
    frequency = jnp.arange(2 * block_count, dtype=jnp.int32)
    block_index = jnp.arange(block_count, dtype=jnp.int32)
    cos_table, sin_table = phase_table(frequency[:, None] * block_index[None, :], 2 * block_count)
    real_part = contract("ca,arx->crx", cos_table, signal)
    imag_part = -contract("ca,arx->crx", sin_table, signal)
    row_index = row_first + jnp.arange(row_count, dtype=jnp.int32)
    cos_twist, sin_twist = phase_table(frequency[:, None] * row_index[None, :], padded)
    cos_twist = cos_twist[:, :, None]
    sin_twist = sin_twist[:, :, None]
    return (
        real_part * cos_twist + imag_part * sin_twist,
        imag_part * cos_twist - real_part * sin_twist,
    )


def along_rows(real_part, imag_part, direction):
    length = real_part.shape[1]
    indices = jnp.arange(length, dtype=jnp.int32)
    cos_table, sin_table = phase_table(indices[:, None] * indices[None, :], length)
    cos_real = contract("dr,crx->cdx", cos_table, real_part)
    cos_imag = contract("dr,crx->cdx", cos_table, imag_part)
    sin_real = contract("dr,crx->cdx", sin_table, real_part)
    sin_imag = contract("dr,crx->cdx", sin_table, imag_part)
    return (cos_real - direction * sin_imag, cos_imag + direction * sin_real)


def inverse_twist(real_part, imag_part, freq_first, padded):
    frequency = freq_first + jnp.arange(real_part.shape[0], dtype=jnp.int32)
    row_index = jnp.arange(real_part.shape[1], dtype=jnp.int32)
    cos_twist, sin_twist = phase_table(frequency[:, None] * row_index[None, :], padded)
    cos_twist = cos_twist[:, :, None]
    sin_twist = sin_twist[:, :, None]
    return (
        real_part * cos_twist - imag_part * sin_twist,
        imag_part * cos_twist + real_part * sin_twist,
    )


def inverse_blocks(real_part, imag_part, padded):
    block_count = real_part.shape[0] // 2
    block_index = jnp.arange(block_count, dtype=jnp.int32)
    frequency = jnp.arange(2 * block_count, dtype=jnp.int32)
    cos_table, sin_table = phase_table(block_index[:, None] * frequency[None, :], 2 * block_count)
    summed = contract("ac,crx->arx", cos_table, real_part) - contract(
        "ac,crx->arx", sin_table, imag_part
    )
    return summed * (1.0 / padded)


def spectral_products(conv_real, conv_imag, gated_real, gated_imag, filter_real, filter_imag):
    back_real = conv_real * filter_real + conv_imag * filter_imag
    back_imag = conv_imag * filter_real - conv_real * filter_imag
    fold_real = conv_real * gated_real + conv_imag * gated_imag
    fold_imag = conv_imag * gated_real - conv_real * gated_imag
    return (back_real, back_imag, fold_real, fold_imag)


def spread_body(grad_out, value_branch, key_gate, query_gate, short_weights, long_filters):
    grad_y = grad_out[0]
    tok_rows, columns = grad_y.shape
    devices = lax.axis_size("seq")
    position = lax.axis_index("seq")
    padded = 2 * tok_rows * devices
    key_values = key_gate[0].astype(jnp.float32)
    grad_conv = (query_gate[0].astype(jnp.float32) * grad_y.astype(jnp.float32)).astype(
        jnp.bfloat16
    )
    gated_value = (key_values * value_branch[0].astype(jnp.float32)).astype(jnp.bfloat16)
    per_device = tok_rows // devices
    pieces = (
        lax.all_to_all(grad_conv[None], "seq", split_axis=1, concat_axis=0, tiled=True),
        lax.all_to_all(gated_value[None], "seq", split_axis=1, concat_axis=0, tiled=True),
        lax.all_to_all(long_filters, "seq", split_axis=1, concat_axis=0, tiled=True),
    )
    halves = [
        forward_blocks(piece.astype(jnp.float32), position * per_device, padded) for piece in pieces
    ]
    exchanged = (
        lax.all_to_all(halves[0][0], "seq", split_axis=0, concat_axis=1, tiled=True),
        lax.all_to_all(halves[0][1], "seq", split_axis=0, concat_axis=1, tiled=True),
        lax.all_to_all(halves[1][0], "seq", split_axis=0, concat_axis=1, tiled=True),
        lax.all_to_all(halves[1][1], "seq", split_axis=0, concat_axis=1, tiled=True),
        lax.all_to_all(halves[2][0], "seq", split_axis=0, concat_axis=1, tiled=True),
        lax.all_to_all(halves[2][1], "seq", split_axis=0, concat_axis=1, tiled=True),
    )
    conv_real, conv_imag = along_rows(exchanged[0], exchanged[1], -1.0)
    gated_real, gated_imag = along_rows(exchanged[2], exchanged[3], -1.0)
    filter_real, filter_imag = along_rows(exchanged[4], exchanged[5], -1.0)
    back_real, back_imag, fold_real, fold_imag = spectral_products(
        conv_real, conv_imag, gated_real, gated_imag, filter_real, filter_imag
    )
    pair_count = fold_real.shape[0]
    back_real, back_imag = along_rows(back_real, back_imag, 1.0)
    back_real, back_imag = inverse_twist(back_real, back_imag, position * pair_count, padded)
    fold_real, fold_imag = along_rows(fold_real, fold_imag, 1.0)
    fold_real, fold_imag = inverse_twist(fold_real, fold_imag, position * pair_count, padded)
    returned = (
        lax.all_to_all(back_real, "seq", split_axis=1, concat_axis=0, tiled=True),
        lax.all_to_all(back_imag, "seq", split_axis=1, concat_axis=0, tiled=True),
        lax.all_to_all(fold_real, "seq", split_axis=1, concat_axis=0, tiled=True),
        lax.all_to_all(fold_imag, "seq", split_axis=1, concat_axis=0, tiled=True),
    )
    settled = (
        lax.all_to_all(
            inverse_blocks(returned[0], returned[1], padded),
            "seq",
            split_axis=0,
            concat_axis=1,
            tiled=True,
        ),
        lax.all_to_all(
            inverse_blocks(returned[2], returned[3], padded),
            "seq",
            split_axis=0,
            concat_axis=1,
            tiled=True,
        ),
    )
    grad_gated = settled[0][0]
    grad_filter = settled[1][0]
    grad_value = key_values * grad_gated
    next_rim = from_behind(grad_value[:2], "seq", -1)
    longer = jnp.concatenate([grad_value, next_rim], axis=0)
    weights = short_weights[0]
    grad_input = (
        weights[0] * longer[:tok_rows]
        + weights[1] * longer[1 : tok_rows + 1]
        + weights[2] * longer[2:]
    )
    passed = shifted(grad_input.astype(jnp.bfloat16)[None], "pipe", -1)
    return (passed, grad_filter[None])


LANES = 128
RIM = 16
PARTS = 2
MESH = pl.DeviceIdType.MESH


def half_step_tables(tokens, devices):
    half = tokens // 2
    odd = 2 * np.arange(half, dtype=np.int64)[:, None] + 1
    turns = (odd * np.arange(tokens, dtype=np.int64)[None, :]) % (4 * tokens)
    angles = turns * (2.0 * np.pi / (4 * tokens))
    part = half // PARTS
    share = tokens // devices // 2
    forward, inverse = [], []
    for parity in range(2):
        cosines, sines = np.cos(angles[:, parity::2]), np.sin(angles[:, parity::2])
        for first in range(0, half, part):
            forward.append(pair(np.concatenate([cosines[first : first + part], sines[first : first + part]])))
        back = np.concatenate([cosines, sines]).T
        back = np.concatenate([back, np.zeros((RIM, 2 * half))])
        for first in range(0, half, share):
            inverse.append(pair(back[first : first + share + RIM]))
    return (
        np.stack(forward).reshape(2, PARTS, 4 * part, half),
        np.stack(inverse).reshape(2, devices, 2 * (share + RIM), 2 * half),
    )


def pair(table):
    high = table.astype(jnp.bfloat16)
    low = (table - high.astype(np.float64)).astype(jnp.bfloat16)
    return np.concatenate([high, low])


def relay_kernel(
    devices, go_hbm, vb_hbm, kg_hbm, qg_hbm, sw, lf, fwd_hbm, inv_hbm,
    passed, fold_out,
    go, vb, kg, qg,
    conv_src, gated_src, filt_src, both_all, gated_all, fwd, inv, mixed, woven,
    spec_both, spec_gated, packed, back_src, fold_src, back_got, fold_got, key_got, weight_got,
    load_sem, filt_sem, own_sem, send_sem, recv_sem, back_send, back_recv, side_send, side_recv,
):
    rows = go.shape[0]
    tokens = rows * devices
    half = tokens // 2
    share = rows // 2
    pipe = lax.axis_index("pipe")
    me = lax.axis_index("seq")
    other = 1 - pipe
    far_first = sorted(range(1, devices), key=lambda d: (abs(2 * d - devices), d))

    loads = []
    for i, (source, target) in enumerate(
        ((go_hbm.at[0], go), (qg_hbm.at[0], qg), (kg_hbm.at[0], kg), (vb_hbm.at[0], vb), (fwd_hbm, fwd), (inv_hbm, inv))
    ):
        copy = pltpu.make_async_copy(source, target, load_sem.at[i])
        copy.start()
        loads.append(copy)

    filt_loads = []
    for block in range(devices):
        copy = pltpu.make_async_copy(
            lf.at[0, :, pl.ds(block * LANES, LANES)], filt_src.at[block], filt_sem.at[block]
        )
        copy.start()
        filt_loads.append(copy)

    def gate(left, right, target):
        for block in range(devices):
            columns = pl.ds(block * LANES, LANES)
            value = left[:, columns].astype(jnp.float32) * right[:, columns].astype(jnp.float32)
            target[block] = value.astype(jnp.bfloat16)

    def peer(distance):
        return lax.rem(me + distance, devices)

    def behind(distance):
        return lax.rem(me + devices - distance, devices)

    barrier = pltpu.get_barrier_semaphore()
    for distance in range(devices):
        if distance:
            pl.semaphore_signal(
                barrier, inc=1, device_id={"pipe": pipe, "seq": peer(distance)}, device_id_type=MESH
            )
        pl.semaphore_signal(
            barrier, inc=1, device_id={"pipe": other, "seq": peer(distance)}, device_id_type=MESH
        )
    loads[0].wait()
    loads[1].wait()
    gate(qg, go, conv_src)
    for copy in filt_loads:
        copy.wait()
    pl.semaphore_wait(barrier, 2 * devices - 1)

    def lanes_of(device):
        return pl.ds(pl.multiple_of(device * LANES, LANES), LANES)

    def rows_of(device):
        return pl.ds(pl.multiple_of(device * rows, rows), rows)

    first, second = pl.ds(0, LANES), pl.ds(LANES, LANES)

    def scatter(kind, source, target, columns, before=()):
        copies = []
        for i, distance in enumerate(far_first):
            if before:
                before[i].wait_send()
            copy = pltpu.make_async_remote_copy(
                src_ref=source.at[peer(distance)],
                dst_ref=target.at[rows_of(me), columns],
                send_sem=send_sem.at[kind, distance],
                recv_sem=recv_sem.at[kind, distance],
                device_id={"pipe": pipe, "seq": peer(distance)},
                device_id_type=MESH,
            )
            copy.start()
            copies.append(copy)
        own = pltpu.make_async_copy(
            source.at[me], target.at[rows_of(me), columns], own_sem.at[kind]
        )
        own.start()
        return own, copies

    def landed(group):
        own, copies = group
        own.wait()
        for copy in copies:
            copy.wait_recv()

    filt_group = scatter(0, filt_src, both_all, first)
    conv_group = scatter(1, conv_src, both_all, second)
    loads[2].wait()
    loads[3].wait()
    gate(kg, vb, gated_src)
    side = []
    for i, (source, target, at) in enumerate(
        (
            (kg, key_got.at[pl.ds(0, rows)], me),
            (kg.at[pl.ds(0, RIM)], key_got.at[pl.ds(rows, RIM)], behind(1)),
            (sw, weight_got, me),
        )
    ):
        copy = pltpu.make_async_remote_copy(
            src_ref=source, dst_ref=target, send_sem=side_send.at[i], recv_sem=side_recv.at[i],
            device_id={"pipe": other, "seq": at}, device_id_type=MESH,
        )
        copy.start()
        side.append(copy)

    gated_group = scatter(2, gated_src, gated_all, first, filt_group[1])
    part = half // PARTS

    def transform(signal, target):
        width = signal.shape[1]
        evens, odds = [], []
        for at in range(0, width, LANES):
            mixed[...] = signal[:, pl.ds(at, LANES)].astype(jnp.float32)
            evens.append(mixed[pl.ds(0, half, stride=2), :].astype(jnp.bfloat16))
            odds.append(mixed[pl.ds(1, half, stride=2), :].astype(jnp.bfloat16))
        evens, odds = jnp.concatenate(evens, axis=1), jnp.concatenate(odds, axis=1)
        for i in range(PARTS):
            even = jnp.dot(fwd[0, i], evens, preferred_element_type=jnp.float32)
            even = even[: 2 * part] + even[2 * part :]
            odd = jnp.dot(fwd[1, i], odds, preferred_element_type=jnp.float32)
            odd = odd[: 2 * part] + odd[2 * part :]
            at = pl.ds(i * part, part)
            target[0, at, :] = even[:part] + odd[:part]
            target[1, at, :] = even[:part] - odd[:part]
            target[2, at, :] = odd[part:] + even[part:]
            target[3, at, :] = odd[part:] - even[part:]

    def pack(kind, parity, at, value):
        high = value.astype(jnp.bfloat16)
        packed[kind, parity, at, first] = high
        packed[kind, parity, at, second] = (value - high.astype(jnp.float32)).astype(jnp.bfloat16)

    def multiply(kind, spec_other):
        chunk = 64

        @pl.loop(0, half // chunk)
        def _(step):
            at = pl.ds(pl.multiple_of(step * chunk, chunk), chunk)
            low = pl.ds(pl.multiple_of(half + step * chunk, chunk), chunk)
            scale = 1.0 / tokens
            alike, cross = [], []
            for mirror in range(2):
                conv_cos = spec_both[mirror, at, second] * scale
                conv_sin = spec_both[2 + mirror, at, second] * scale
                other_cos, other_sin = spec_other[mirror, at, first], spec_other[2 + mirror, at, first]
                alike.append(conv_cos * other_cos + conv_sin * other_sin)
                cross.append(conv_sin * other_cos - conv_cos * other_sin)
            pack(kind, 0, at, alike[0] + alike[1])
            pack(kind, 0, low, cross[0] - cross[1])
            pack(kind, 1, at, alike[0] - alike[1])
            pack(kind, 1, low, cross[0] + cross[1])

    def invert(kind, block):
        for parity in range(2):
            wide = jnp.dot(inv[parity, block], packed[kind, parity], preferred_element_type=jnp.float32)
            wide = wide[: share + RIM] + wide[share + RIM :]
            wide = wide[:, :LANES] + wide[:, LANES:]
            woven[pl.ds(parity, share + RIM, stride=2), :] = wide

    def send_back(distance):
        invert(0, peer(distance))
        back_src[distance] = woven[pl.ds(0, rows + RIM), :].astype(jnp.bfloat16)
        copy = pltpu.make_async_remote_copy(
            src_ref=back_src.at[distance],
            dst_ref=back_got.at[me],
            send_sem=back_send.at[distance],
            recv_sem=back_recv.at[distance],
            device_id={"pipe": other, "seq": peer(distance)},
            device_id_type=MESH,
        )
        copy.start()
        return copy

    def send_fold(distance):
        invert(1, peer(distance))
        fold_src[distance] = woven[pl.ds(0, rows), :].astype(jnp.bfloat16)
        copy = pltpu.make_async_remote_copy(
            src_ref=fold_src.at[distance],
            dst_ref=fold_got.at[me],
            send_sem=send_sem.at[3, distance],
            recv_sem=recv_sem.at[3, distance],
            device_id={"pipe": pipe, "seq": peer(distance)},
            device_id_type=MESH,
        )
        copy.start()
        return copy

    loads[4].wait()
    landed(filt_group)
    landed(conv_group)
    transform(both_all, spec_both)
    multiply(0, spec_both)
    loads[5].wait()
    backs = [send_back(distance) for distance in far_first]
    landed(gated_group)
    transform(gated_all, spec_gated)
    multiply(1, spec_gated)
    folds = [send_fold(distance) for distance in far_first]
    backs.append(send_back(0))
    invert(1, me)
    fold_out[0, :, lanes_of(me)] = woven[pl.ds(0, rows), :]

    for copy in side:
        copy.wait_recv()
    for copy, distance in zip(backs, far_first + [0]):
        copy.wait_recv()
        columns = lanes_of(behind(distance))
        value = key_got[:, columns].astype(jnp.float32) * back_got[behind(distance)].astype(jnp.float32)
        extent = rows + RIM
        total = weight_got[0, :, columns] * value
        total += weight_got[1, :, columns] * pltpu.roll(value, extent - 1, 0)
        total += weight_got[2, :, columns] * pltpu.roll(value, extent - 2, 0)
        passed[0, :, columns] = total[:rows].astype(jnp.bfloat16)
    for copy, distance in zip(folds, far_first):
        copy.wait_recv()
        fold_out[0, :, lanes_of(behind(distance))] = fold_got[behind(distance)].astype(jnp.float32)
    for copy in conv_group[1] + gated_group[1] + side + backs + folds:
        copy.wait_send()


def relay_body(grad_out, value_branch, key_gate, query_gate, short_weights, long_filters):
    _, rows, columns = grad_out.shape
    devices = lax.axis_size("seq")
    tokens = rows * devices
    tables = [jnp.asarray(table) for table in half_step_tables(tokens, devices)]
    vmem = pl.BlockSpec(memory_space=pltpu.VMEM)
    anywhere = pl.BlockSpec(memory_space=pltpu.HBM)
    half, full = jnp.bfloat16, jnp.float32
    return pl.pallas_call(
        functools.partial(relay_kernel, devices),
        out_shape=(
            pltpu.VMEM((1, rows, columns), half),
            pltpu.VMEM((1, rows, columns), full),
        ),
        in_specs=[anywhere] * 8,
        out_specs=(vmem, vmem),
        scratch_shapes=[pltpu.VMEM((rows, columns), half)] * 4
        + [pltpu.VMEM((devices, rows, LANES), half)] * 3
        + [
            pltpu.VMEM((tokens, 2 * LANES), half),
            pltpu.VMEM((tokens, LANES), half),
            pltpu.VMEM(tables[0].shape, half),
            pltpu.VMEM(tables[1].shape, half),
            pltpu.VMEM((tokens, LANES), full),
            pltpu.VMEM((rows + 2 * RIM, LANES), full),
            pltpu.VMEM((4, tokens // 2, 2 * LANES), full),
            pltpu.VMEM((4, tokens // 2, LANES), full),
            pltpu.VMEM((2, 2, tokens, 2 * LANES), half),
            pltpu.VMEM((devices, rows + RIM, LANES), half),
            pltpu.VMEM((devices, rows, LANES), half),
            pltpu.VMEM((devices, rows + RIM, LANES), half),
            pltpu.VMEM((devices, rows, LANES), half),
            pltpu.VMEM((rows + RIM, columns), half),
            pltpu.VMEM((3, 1, columns), full),
            pltpu.SemaphoreType.DMA((6,)),
            pltpu.SemaphoreType.DMA((devices,)),
            pltpu.SemaphoreType.DMA((3,)),
            pltpu.SemaphoreType.DMA((4, devices)),
            pltpu.SemaphoreType.DMA((4, devices)),
            pltpu.SemaphoreType.DMA((devices,)),
            pltpu.SemaphoreType.DMA((devices,)),
            pltpu.SemaphoreType.DMA((3,)),
            pltpu.SemaphoreType.DMA((3,)),
        ],
        compiler_params=pltpu.CompilerParams(
            collective_id=0, has_side_effects=True, vmem_limit_bytes=62 * 2**20
        ),
        cost_estimate=pl.CostEstimate(
            flops=16 * tokens * tokens * LANES, bytes_accessed=10 * tokens * tokens, transcendentals=0
        ),
    )(
        grad_out, value_branch, key_gate, query_gate,
        jnp.transpose(short_weights, (1, 0, 2)), long_filters, *tables,
    )


def solution(mesh):
    placed = (
        P("pipe", "seq", "chan"),
        P("pipe", "seq", "chan"),
        P("pipe", "seq", "chan"),
        P("pipe", "seq", "chan"),
        P("pipe", None, "chan"),
        P("pipe", "seq", "chan"),
    )

    def run(*arrays):
        _, tokens, channels = arrays[0].shape
        devices = mesh.shape["seq"]
        fits = (
            mesh.shape["pipe"] == 2
            and devices > 1
            and channels == mesh.shape["chan"] * devices * LANES
            and tokens <= 1024
            and tokens % (2 * devices * RIM) == 0
            and tokens % (2 * LANES) == 0
        )
        return jax.shard_map(
            relay_body if fits else spread_body,
            mesh=mesh,
            in_specs=placed,
            out_specs=(P("pipe", "seq", "chan"), P("pipe", "seq", "chan")),
            check_vma=False,
        )(*arrays)

    return run
```

```python
import functools
import math

import jax
import jax.numpy as jnp
import numpy as np
from jax import lax
from jax.experimental import pallas as pl
from jax.experimental.pallas import tpu as pltpu
from jax.sharding import PartitionSpec as P


def from_behind(value, axis, by):
    devices = lax.axis_size(axis)
    pairs = [(i, i + by) for i in range(devices) if 0 <= i + by < devices]
    return lax.ppermute(value, axis, pairs)


def shifted(block, axis, distance):
    devices = range(lax.axis_size(axis))
    route = [((i - distance) % len(devices), i) for i in devices]
    return lax.ppermute(block, axis, route)


def phase_table(product, modulus):
    angles = (product % modulus).astype(jnp.float32) * (2.0 * math.pi / modulus)
    return (jnp.cos(angles), jnp.sin(angles))


def contract(form, table, values):
    return jnp.einsum(form, table, values, precision=lax.Precision.HIGHEST)


def forward_blocks(signal, row_first, padded):
    block_count = signal.shape[0]
    row_count = signal.shape[1]
    frequency = jnp.arange(2 * block_count, dtype=jnp.int32)
    block_index = jnp.arange(block_count, dtype=jnp.int32)
    cos_table, sin_table = phase_table(frequency[:, None] * block_index[None, :], 2 * block_count)
    real_part = contract("ca,arx->crx", cos_table, signal)
    imag_part = -contract("ca,arx->crx", sin_table, signal)
    row_index = row_first + jnp.arange(row_count, dtype=jnp.int32)
    cos_twist, sin_twist = phase_table(frequency[:, None] * row_index[None, :], padded)
    cos_twist = cos_twist[:, :, None]
    sin_twist = sin_twist[:, :, None]
    return (
        real_part * cos_twist + imag_part * sin_twist,
        imag_part * cos_twist - real_part * sin_twist,
    )


def along_rows(real_part, imag_part, direction):
    length = real_part.shape[1]
    indices = jnp.arange(length, dtype=jnp.int32)
    cos_table, sin_table = phase_table(indices[:, None] * indices[None, :], length)
    cos_real = contract("dr,crx->cdx", cos_table, real_part)
    cos_imag = contract("dr,crx->cdx", cos_table, imag_part)
    sin_real = contract("dr,crx->cdx", sin_table, real_part)
    sin_imag = contract("dr,crx->cdx", sin_table, imag_part)
    return (cos_real - direction * sin_imag, cos_imag + direction * sin_real)


def inverse_twist(real_part, imag_part, freq_first, padded):
    frequency = freq_first + jnp.arange(real_part.shape[0], dtype=jnp.int32)
    row_index = jnp.arange(real_part.shape[1], dtype=jnp.int32)
    cos_twist, sin_twist = phase_table(frequency[:, None] * row_index[None, :], padded)
    cos_twist = cos_twist[:, :, None]
    sin_twist = sin_twist[:, :, None]
    return (
        real_part * cos_twist - imag_part * sin_twist,
        imag_part * cos_twist + real_part * sin_twist,
    )


def inverse_blocks(real_part, imag_part, padded):
    block_count = real_part.shape[0] // 2
    block_index = jnp.arange(block_count, dtype=jnp.int32)
    frequency = jnp.arange(2 * block_count, dtype=jnp.int32)
    cos_table, sin_table = phase_table(block_index[:, None] * frequency[None, :], 2 * block_count)
    summed = contract("ac,crx->arx", cos_table, real_part) - contract(
        "ac,crx->arx", sin_table, imag_part
    )
    return summed * (1.0 / padded)


def spectral_products(conv_real, conv_imag, gated_real, gated_imag, filter_real, filter_imag):
    back_real = conv_real * filter_real + conv_imag * filter_imag
    back_imag = conv_imag * filter_real - conv_real * filter_imag
    fold_real = conv_real * gated_real + conv_imag * gated_imag
    fold_imag = conv_imag * gated_real - conv_real * gated_imag
    return (back_real, back_imag, fold_real, fold_imag)


def spread_body(grad_out, value_branch, key_gate, query_gate, short_weights, long_filters):
    grad_y = grad_out[0]
    tok_rows, columns = grad_y.shape
    devices = lax.axis_size("seq")
    position = lax.axis_index("seq")
    padded = 2 * tok_rows * devices
    key_values = key_gate[0].astype(jnp.float32)
    grad_conv = (query_gate[0].astype(jnp.float32) * grad_y.astype(jnp.float32)).astype(
        jnp.bfloat16
    )
    gated_value = (key_values * value_branch[0].astype(jnp.float32)).astype(jnp.bfloat16)
    per_device = tok_rows // devices
    pieces = (
        lax.all_to_all(grad_conv[None], "seq", split_axis=1, concat_axis=0, tiled=True),
        lax.all_to_all(gated_value[None], "seq", split_axis=1, concat_axis=0, tiled=True),
        lax.all_to_all(long_filters, "seq", split_axis=1, concat_axis=0, tiled=True),
    )
    halves = [
        forward_blocks(piece.astype(jnp.float32), position * per_device, padded) for piece in pieces
    ]
    exchanged = (
        lax.all_to_all(halves[0][0], "seq", split_axis=0, concat_axis=1, tiled=True),
        lax.all_to_all(halves[0][1], "seq", split_axis=0, concat_axis=1, tiled=True),
        lax.all_to_all(halves[1][0], "seq", split_axis=0, concat_axis=1, tiled=True),
        lax.all_to_all(halves[1][1], "seq", split_axis=0, concat_axis=1, tiled=True),
        lax.all_to_all(halves[2][0], "seq", split_axis=0, concat_axis=1, tiled=True),
        lax.all_to_all(halves[2][1], "seq", split_axis=0, concat_axis=1, tiled=True),
    )
    conv_real, conv_imag = along_rows(exchanged[0], exchanged[1], -1.0)
    gated_real, gated_imag = along_rows(exchanged[2], exchanged[3], -1.0)
    filter_real, filter_imag = along_rows(exchanged[4], exchanged[5], -1.0)
    back_real, back_imag, fold_real, fold_imag = spectral_products(
        conv_real, conv_imag, gated_real, gated_imag, filter_real, filter_imag
    )
    pair_count = fold_real.shape[0]
    back_real, back_imag = along_rows(back_real, back_imag, 1.0)
    back_real, back_imag = inverse_twist(back_real, back_imag, position * pair_count, padded)
    fold_real, fold_imag = along_rows(fold_real, fold_imag, 1.0)
    fold_real, fold_imag = inverse_twist(fold_real, fold_imag, position * pair_count, padded)
    returned = (
        lax.all_to_all(back_real, "seq", split_axis=1, concat_axis=0, tiled=True),
        lax.all_to_all(back_imag, "seq", split_axis=1, concat_axis=0, tiled=True),
        lax.all_to_all(fold_real, "seq", split_axis=1, concat_axis=0, tiled=True),
        lax.all_to_all(fold_imag, "seq", split_axis=1, concat_axis=0, tiled=True),
    )
    settled = (
        lax.all_to_all(
            inverse_blocks(returned[0], returned[1], padded),
            "seq",
            split_axis=0,
            concat_axis=1,
            tiled=True,
        ),
        lax.all_to_all(
            inverse_blocks(returned[2], returned[3], padded),
            "seq",
            split_axis=0,
            concat_axis=1,
            tiled=True,
        ),
    )
    grad_gated = settled[0][0]
    grad_filter = settled[1][0]
    grad_value = key_values * grad_gated
    next_rim = from_behind(grad_value[:2], "seq", -1)
    longer = jnp.concatenate([grad_value, next_rim], axis=0)
    weights = short_weights[0]
    grad_input = (
        weights[0] * longer[:tok_rows]
        + weights[1] * longer[1 : tok_rows + 1]
        + weights[2] * longer[2:]
    )
    passed = shifted(grad_input.astype(jnp.bfloat16)[None], "pipe", -1)
    return (passed, grad_filter[None])


LANES = 128
RIM = 16
PARTS = 2
SPLIT = 4
MESH = pl.DeviceIdType.MESH


def half_step_tables(tokens, devices):
    half = tokens // 2
    odd = 2 * np.arange(half, dtype=np.int64)[:, None] + 1
    turns = (odd * np.arange(tokens, dtype=np.int64)[None, :]) % (4 * tokens)
    angles = turns * (2.0 * np.pi / (4 * tokens))
    part = half // PARTS
    share = tokens // devices // 2
    forward, inverse = [], []
    for parity in range(2):
        cosines, sines = np.cos(angles[:, parity::2]), np.sin(angles[:, parity::2])
        for first in range(0, half, part):
            forward.append(pair(np.concatenate([cosines[first : first + part], sines[first : first + part]])))
        back = np.concatenate([cosines, sines]).T
        back = np.concatenate([back, np.zeros((RIM, 2 * half))])
        for first in range(0, half, share):
            inverse.append(pair(back[first : first + share + RIM]))
    return (
        np.stack(forward).reshape(2, PARTS, 4 * part, half),
        np.stack(inverse).reshape(2, devices, 2 * (share + RIM), 2 * half),
    )


def pair(table):
    high = table.astype(jnp.bfloat16)
    low = (table - high.astype(np.float64)).astype(jnp.bfloat16)
    return np.concatenate([high, low])


def relay_kernel(
    devices, go_hbm, vb_hbm, kg_hbm, qg_hbm, sw, lf, fwd_hbm, inv_hbm,
    passed, fold_out,
    go, vb, kg, qg,
    conv_src, gated_src, filt_src, both_all, gated_all, fwd, inv, mixed, woven,
    spec_both, spec_gated, packed, back_src, fold_src, back_got, fold_got, key_got, weight_got,
    load_sem, filt_sem, own_sem, send_sem, recv_sem, back_send, back_recv, side_send, side_recv,
):
    rows = go.shape[0]
    tokens = rows * devices
    half = tokens // 2
    share = rows // 2
    pipe = lax.axis_index("pipe")
    me = lax.axis_index("seq")
    other = 1 - pipe
    far_first = sorted(range(1, devices), key=lambda d: (abs(2 * d - devices), d))

    loads = []
    for i, (source, target) in enumerate(
        ((go_hbm.at[0], go), (qg_hbm.at[0], qg), (kg_hbm.at[0], kg), (vb_hbm.at[0], vb), (fwd_hbm, fwd), (inv_hbm, inv))
    ):
        copy = pltpu.make_async_copy(source, target, load_sem.at[i])
        copy.start()
        loads.append(copy)

    filt_loads = []
    for block in range(devices):
        copy = pltpu.make_async_copy(
            lf.at[0, :, pl.ds(block * LANES, LANES)], filt_src.at[block], filt_sem.at[block]
        )
        copy.start()
        filt_loads.append(copy)

    def gate(left, right, target):
        for block in range(devices):
            columns = pl.ds(block * LANES, LANES)
            value = left[:, columns].astype(jnp.float32) * right[:, columns].astype(jnp.float32)
            target[block] = value.astype(jnp.bfloat16)

    def peer(distance):
        return lax.rem(me + distance, devices)

    def behind(distance):
        return lax.rem(me + devices - distance, devices)

    barrier = pltpu.get_barrier_semaphore()
    for distance in range(devices):
        if distance:
            pl.semaphore_signal(
                barrier, inc=1, device_id={"pipe": pipe, "seq": peer(distance)}, device_id_type=MESH
            )
        pl.semaphore_signal(
            barrier, inc=1, device_id={"pipe": other, "seq": peer(distance)}, device_id_type=MESH
        )
    loads[0].wait()
    loads[1].wait()
    gate(qg, go, conv_src)
    for copy in filt_loads:
        copy.wait()
    pl.semaphore_wait(barrier, 2 * devices - 1)

    def lanes_of(device):
        return pl.ds(pl.multiple_of(device * LANES, LANES), LANES)

    def rows_of(device):
        return pl.ds(pl.multiple_of(device * rows, rows), rows)

    first, second = pl.ds(0, LANES), pl.ds(LANES, LANES)

    def scatter(kind, source, target, columns):
        copies = []
        for distance in far_first:
            copy = pltpu.make_async_remote_copy(
                src_ref=source.at[peer(distance)],
                dst_ref=target.at[rows_of(me), columns],
                send_sem=send_sem.at[kind, distance],
                recv_sem=recv_sem.at[kind, distance],
                device_id={"pipe": pipe, "seq": peer(distance)},
                device_id_type=MESH,
            )
            copy.start()
            copies.append(copy)
        own = pltpu.make_async_copy(
            source.at[me], target.at[rows_of(me), columns], own_sem.at[kind]
        )
        own.start()
        return own, copies

    def landed(group):
        own, copies = group
        own.wait()
        for copy in copies:
            copy.wait_recv()

    filt_group = scatter(0, filt_src, both_all, first)
    conv_group = scatter(1, conv_src, both_all, second)
    loads[2].wait()
    loads[3].wait()
    gate(kg, vb, gated_src)
    side = []
    for i, (source, target, at) in enumerate(
        (
            (kg, key_got.at[pl.ds(0, rows)], me),
            (kg.at[pl.ds(0, RIM)], key_got.at[pl.ds(rows, RIM)], behind(1)),
            (sw, weight_got, me),
        )
    ):
        copy = pltpu.make_async_remote_copy(
            src_ref=source, dst_ref=target, send_sem=side_send.at[i], recv_sem=side_recv.at[i],
            device_id={"pipe": other, "seq": at}, device_id_type=MESH,
        )
        copy.start()
        side.append(copy)

    gated_group = scatter(2, gated_src, gated_all, first)
    part = half // PARTS

    def transform(signal, target):
        width = signal.shape[1]
        evens, odds = [], []
        for at in range(0, width, LANES):
            mixed[...] = signal[:, pl.ds(at, LANES)].astype(jnp.float32)
            evens.append(mixed[pl.ds(0, half, stride=2), :].astype(jnp.bfloat16))
            odds.append(mixed[pl.ds(1, half, stride=2), :].astype(jnp.bfloat16))
        evens, odds = jnp.concatenate(evens, axis=1), jnp.concatenate(odds, axis=1)
        for i in range(PARTS):
            even = jnp.dot(fwd[0, i], evens, preferred_element_type=jnp.float32)
            even = even[: 2 * part] + even[2 * part :]
            odd = jnp.dot(fwd[1, i], odds, preferred_element_type=jnp.float32)
            odd = odd[: 2 * part] + odd[2 * part :]
            at = pl.ds(i * part, part)
            target[0, at, :] = even[:part] + odd[:part]
            target[1, at, :] = even[:part] - odd[:part]
            target[2, at, :] = odd[part:] + even[part:]
            target[3, at, :] = odd[part:] - even[part:]

    def pack(kind, parity, at, value):
        high = value.astype(jnp.bfloat16)
        packed[kind, parity, at, first] = high
        packed[kind, parity, at, second] = (value - high.astype(jnp.float32)).astype(jnp.bfloat16)

    def multiply(kind, spec_other):
        chunk = 64

        @pl.loop(0, half // chunk)
        def _(step):
            at = pl.ds(pl.multiple_of(step * chunk, chunk), chunk)
            low = pl.ds(pl.multiple_of(half + step * chunk, chunk), chunk)
            scale = 1.0 / tokens
            alike, cross = [], []
            for mirror in range(2):
                conv_cos = spec_both[mirror, at, second] * scale
                conv_sin = spec_both[2 + mirror, at, second] * scale
                other_cos, other_sin = spec_other[mirror, at, first], spec_other[2 + mirror, at, first]
                alike.append(conv_cos * other_cos + conv_sin * other_sin)
                cross.append(conv_sin * other_cos - conv_cos * other_sin)
            pack(kind, 0, at, alike[0] + alike[1])
            pack(kind, 0, low, cross[0] - cross[1])
            pack(kind, 1, at, alike[0] - alike[1])
            pack(kind, 1, low, cross[0] + cross[1])

    def invert(kind, block):
        for parity in range(2):
            wide = jnp.dot(inv[parity, block], packed[kind, parity], preferred_element_type=jnp.float32)
            wide = wide[: share + RIM] + wide[share + RIM :]
            wide = wide[:, :LANES] + wide[:, LANES:]
            woven[pl.ds(parity, share + RIM, stride=2), :] = wide

    def send_back(distance):
        invert(0, peer(distance))
        back_src[distance] = woven[pl.ds(0, rows + RIM), :].astype(jnp.bfloat16)
        copy = pltpu.make_async_remote_copy(
            src_ref=back_src.at[distance],
            dst_ref=back_got.at[me],
            send_sem=back_send.at[distance],
            recv_sem=back_recv.at[distance],
            device_id={"pipe": other, "seq": peer(distance)},
            device_id_type=MESH,
        )
        copy.start()
        return copy

    def send_fold(distance):
        invert(1, peer(distance))
        fold_src[distance] = woven[pl.ds(0, rows), :].astype(jnp.bfloat16)
        copy = pltpu.make_async_remote_copy(
            src_ref=fold_src.at[distance],
            dst_ref=fold_got.at[me],
            send_sem=send_sem.at[3, distance],
            recv_sem=recv_sem.at[3, distance],
            device_id={"pipe": pipe, "seq": peer(distance)},
            device_id_type=MESH,
        )
        copy.start()
        return copy

    loads[4].wait()
    landed(filt_group)
    landed(conv_group)
    transform(both_all, spec_both)
    multiply(0, spec_both)
    loads[5].wait()
    backs = [send_back(distance) for distance in far_first]
    landed(gated_group)
    transform(gated_all, spec_gated)
    multiply(1, spec_gated)
    folds = [send_fold(distance) for distance in far_first]
    backs.append(send_back(0))
    invert(1, me)
    fold_out[0, :, lanes_of(me)] = woven[pl.ds(0, rows), :]

    for copy in side:
        copy.wait_recv()
    for copy, distance in zip(backs, far_first + [0]):
        copy.wait_recv()
        columns = lanes_of(behind(distance))
        value = key_got[:, columns].astype(jnp.float32) * back_got[behind(distance)].astype(jnp.float32)
        extent = rows + RIM
        total = weight_got[0, :, columns] * value
        total += weight_got[1, :, columns] * pltpu.roll(value, extent - 1, 0)
        total += weight_got[2, :, columns] * pltpu.roll(value, extent - 2, 0)
        passed[0, :, columns] = total[:rows].astype(jnp.bfloat16)
    for copy, distance in zip(folds, far_first):
        copy.wait_recv()
        fold_out[0, :, lanes_of(behind(distance))] = fold_got[behind(distance)].astype(jnp.float32)
    for copy in filt_group[1] + conv_group[1] + gated_group[1] + side + backs + folds:
        copy.wait_send()


def relay_body(grad_out, value_branch, key_gate, query_gate, short_weights, long_filters):
    _, rows, columns = grad_out.shape
    devices = lax.axis_size("seq")
    tokens = rows * devices
    tables = [jnp.asarray(table) for table in half_step_tables(tokens, devices)]
    vmem = pl.BlockSpec(memory_space=pltpu.VMEM)
    anywhere = pl.BlockSpec(memory_space=pltpu.HBM)
    half, full = jnp.bfloat16, jnp.float32
    passed, fold = pl.pallas_call(
        functools.partial(relay_kernel, devices),
        out_shape=(
            pltpu.VMEM((1, rows, columns), half),
            pltpu.VMEM((1, rows, columns), full),
        ),
        in_specs=[anywhere] * 8,
        out_specs=(vmem, vmem),
        scratch_shapes=[pltpu.VMEM((rows, columns), half)] * 4
        + [pltpu.VMEM((devices, rows, LANES), half)] * 3
        + [
            pltpu.VMEM((tokens, 2 * LANES), half),
            pltpu.VMEM((tokens, LANES), half),
            pltpu.VMEM(tables[0].shape, half),
            pltpu.VMEM(tables[1].shape, half),
            pltpu.VMEM((tokens, LANES), full),
            pltpu.VMEM((rows + 2 * RIM, LANES), full),
            pltpu.VMEM((4, tokens // 2, 2 * LANES), full),
            pltpu.VMEM((4, tokens // 2, LANES), full),
            pltpu.VMEM((2, 2, tokens, 2 * LANES), half),
            pltpu.VMEM((devices, rows + RIM, LANES), half),
            pltpu.VMEM((devices, rows, LANES), half),
            pltpu.VMEM((devices, rows + RIM, LANES), half),
            pltpu.VMEM((devices, rows, LANES), half),
            pltpu.VMEM((rows + RIM, columns), half),
            pltpu.VMEM((3, 1, columns), full),
            pltpu.SemaphoreType.DMA((6,)),
            pltpu.SemaphoreType.DMA((devices,)),
            pltpu.SemaphoreType.DMA((3,)),
            pltpu.SemaphoreType.DMA((4, devices)),
            pltpu.SemaphoreType.DMA((4, devices)),
            pltpu.SemaphoreType.DMA((devices,)),
            pltpu.SemaphoreType.DMA((devices,)),
            pltpu.SemaphoreType.DMA((3,)),
            pltpu.SemaphoreType.DMA((3,)),
        ],
        compiler_params=pltpu.CompilerParams(
            collective_id=0, has_side_effects=True, vmem_limit_bytes=62 * 2**20
        ),
        cost_estimate=pl.CostEstimate(
            flops=16 * tokens * tokens * LANES, bytes_accessed=10 * tokens * tokens, transcendentals=0
        ),
    )(
        grad_out, value_branch, key_gate, query_gate,
        jnp.transpose(short_weights, (1, 0, 2)), long_filters, *tables,
    )
    return pl.pallas_call(
        settle_kernel,
        out_shape=(
            jax.ShapeDtypeStruct(passed.shape, half),
            jax.ShapeDtypeStruct(fold.shape, full),
        ),
        in_specs=[vmem, vmem],
        out_specs=(anywhere, anywhere),
        scratch_shapes=[pltpu.SemaphoreType.DMA((2, SPLIT))],
        compiler_params=pltpu.CompilerParams(vmem_limit_bytes=16 * 2**20),
    )(passed, fold)


def settle_kernel(passed, fold, passed_out, fold_out, sem):
    copies = []
    for i, (source, target) in enumerate(((fold, fold_out), (passed, passed_out))):
        step = source.shape[1] // SPLIT
        for j in range(SPLIT):
            at = pl.ds(j * step, step)
            copies.append(pltpu.make_async_copy(source.at[:, at], target.at[:, at], sem.at[i, j]))
    for copy in copies:
        copy.start()
    for copy in copies:
        copy.wait()


def solution(mesh):
    placed = (
        P("pipe", "seq", "chan"),
        P("pipe", "seq", "chan"),
        P("pipe", "seq", "chan"),
        P("pipe", "seq", "chan"),
        P("pipe", None, "chan"),
        P("pipe", "seq", "chan"),
    )

    def run(*arrays):
        _, tokens, channels = arrays[0].shape
        devices = mesh.shape["seq"]
        fits = (
            mesh.shape["pipe"] == 2
            and devices > 1
            and channels == mesh.shape["chan"] * devices * LANES
            and tokens <= 1024
            and tokens % (2 * devices * RIM) == 0
            and tokens % (2 * LANES) == 0
        )
        return jax.shard_map(
            relay_body if fits else spread_body,
            mesh=mesh,
            in_specs=placed,
            out_specs=(P("pipe", "seq", "chan"), P("pipe", "seq", "chan")),
            check_vma=False,
        )(*arrays)

    return run
```

```python
import functools
import math

import jax
import jax.numpy as jnp
import numpy as np
from jax import lax
from jax.experimental import pallas as pl
from jax.experimental.pallas import tpu as pltpu
from jax.sharding import PartitionSpec as P


def from_behind(value, axis, by):
    devices = lax.axis_size(axis)
    pairs = [(i, i + by) for i in range(devices) if 0 <= i + by < devices]
    return lax.ppermute(value, axis, pairs)


def shifted(block, axis, distance):
    devices = range(lax.axis_size(axis))
    route = [((i - distance) % len(devices), i) for i in devices]
    return lax.ppermute(block, axis, route)


def phase_table(product, modulus):
    angles = (product % modulus).astype(jnp.float32) * (2.0 * math.pi / modulus)
    return (jnp.cos(angles), jnp.sin(angles))


def contract(form, table, values):
    return jnp.einsum(form, table, values, precision=lax.Precision.HIGHEST)


def forward_blocks(signal, row_first, padded):
    block_count = signal.shape[0]
    row_count = signal.shape[1]
    frequency = jnp.arange(2 * block_count, dtype=jnp.int32)
    block_index = jnp.arange(block_count, dtype=jnp.int32)
    cos_table, sin_table = phase_table(frequency[:, None] * block_index[None, :], 2 * block_count)
    real_part = contract("ca,arx->crx", cos_table, signal)
    imag_part = -contract("ca,arx->crx", sin_table, signal)
    row_index = row_first + jnp.arange(row_count, dtype=jnp.int32)
    cos_twist, sin_twist = phase_table(frequency[:, None] * row_index[None, :], padded)
    cos_twist = cos_twist[:, :, None]
    sin_twist = sin_twist[:, :, None]
    return (
        real_part * cos_twist + imag_part * sin_twist,
        imag_part * cos_twist - real_part * sin_twist,
    )


def along_rows(real_part, imag_part, direction):
    length = real_part.shape[1]
    indices = jnp.arange(length, dtype=jnp.int32)
    cos_table, sin_table = phase_table(indices[:, None] * indices[None, :], length)
    cos_real = contract("dr,crx->cdx", cos_table, real_part)
    cos_imag = contract("dr,crx->cdx", cos_table, imag_part)
    sin_real = contract("dr,crx->cdx", sin_table, real_part)
    sin_imag = contract("dr,crx->cdx", sin_table, imag_part)
    return (cos_real - direction * sin_imag, cos_imag + direction * sin_real)


def inverse_twist(real_part, imag_part, freq_first, padded):
    frequency = freq_first + jnp.arange(real_part.shape[0], dtype=jnp.int32)
    row_index = jnp.arange(real_part.shape[1], dtype=jnp.int32)
    cos_twist, sin_twist = phase_table(frequency[:, None] * row_index[None, :], padded)
    cos_twist = cos_twist[:, :, None]
    sin_twist = sin_twist[:, :, None]
    return (
        real_part * cos_twist - imag_part * sin_twist,
        imag_part * cos_twist + real_part * sin_twist,
    )


def inverse_blocks(real_part, imag_part, padded):
    block_count = real_part.shape[0] // 2
    block_index = jnp.arange(block_count, dtype=jnp.int32)
    frequency = jnp.arange(2 * block_count, dtype=jnp.int32)
    cos_table, sin_table = phase_table(block_index[:, None] * frequency[None, :], 2 * block_count)
    summed = contract("ac,crx->arx", cos_table, real_part) - contract(
        "ac,crx->arx", sin_table, imag_part
    )
    return summed * (1.0 / padded)


def spectral_products(conv_real, conv_imag, gated_real, gated_imag, filter_real, filter_imag):
    back_real = conv_real * filter_real + conv_imag * filter_imag
    back_imag = conv_imag * filter_real - conv_real * filter_imag
    fold_real = conv_real * gated_real + conv_imag * gated_imag
    fold_imag = conv_imag * gated_real - conv_real * gated_imag
    return (back_real, back_imag, fold_real, fold_imag)


def spread_body(grad_out, value_branch, key_gate, query_gate, short_weights, long_filters):
    grad_y = grad_out[0]
    tok_rows, columns = grad_y.shape
    devices = lax.axis_size("seq")
    position = lax.axis_index("seq")
    padded = 2 * tok_rows * devices
    key_values = key_gate[0].astype(jnp.float32)
    grad_conv = (query_gate[0].astype(jnp.float32) * grad_y.astype(jnp.float32)).astype(
        jnp.bfloat16
    )
    gated_value = (key_values * value_branch[0].astype(jnp.float32)).astype(jnp.bfloat16)
    per_device = tok_rows // devices
    pieces = (
        lax.all_to_all(grad_conv[None], "seq", split_axis=1, concat_axis=0, tiled=True),
        lax.all_to_all(gated_value[None], "seq", split_axis=1, concat_axis=0, tiled=True),
        lax.all_to_all(long_filters, "seq", split_axis=1, concat_axis=0, tiled=True),
    )
    halves = [
        forward_blocks(piece.astype(jnp.float32), position * per_device, padded) for piece in pieces
    ]
    exchanged = (
        lax.all_to_all(halves[0][0], "seq", split_axis=0, concat_axis=1, tiled=True),
        lax.all_to_all(halves[0][1], "seq", split_axis=0, concat_axis=1, tiled=True),
        lax.all_to_all(halves[1][0], "seq", split_axis=0, concat_axis=1, tiled=True),
        lax.all_to_all(halves[1][1], "seq", split_axis=0, concat_axis=1, tiled=True),
        lax.all_to_all(halves[2][0], "seq", split_axis=0, concat_axis=1, tiled=True),
        lax.all_to_all(halves[2][1], "seq", split_axis=0, concat_axis=1, tiled=True),
    )
    conv_real, conv_imag = along_rows(exchanged[0], exchanged[1], -1.0)
    gated_real, gated_imag = along_rows(exchanged[2], exchanged[3], -1.0)
    filter_real, filter_imag = along_rows(exchanged[4], exchanged[5], -1.0)
    back_real, back_imag, fold_real, fold_imag = spectral_products(
        conv_real, conv_imag, gated_real, gated_imag, filter_real, filter_imag
    )
    pair_count = fold_real.shape[0]
    back_real, back_imag = along_rows(back_real, back_imag, 1.0)
    back_real, back_imag = inverse_twist(back_real, back_imag, position * pair_count, padded)
    fold_real, fold_imag = along_rows(fold_real, fold_imag, 1.0)
    fold_real, fold_imag = inverse_twist(fold_real, fold_imag, position * pair_count, padded)
    returned = (
        lax.all_to_all(back_real, "seq", split_axis=1, concat_axis=0, tiled=True),
        lax.all_to_all(back_imag, "seq", split_axis=1, concat_axis=0, tiled=True),
        lax.all_to_all(fold_real, "seq", split_axis=1, concat_axis=0, tiled=True),
        lax.all_to_all(fold_imag, "seq", split_axis=1, concat_axis=0, tiled=True),
    )
    settled = (
        lax.all_to_all(
            inverse_blocks(returned[0], returned[1], padded),
            "seq",
            split_axis=0,
            concat_axis=1,
            tiled=True,
        ),
        lax.all_to_all(
            inverse_blocks(returned[2], returned[3], padded),
            "seq",
            split_axis=0,
            concat_axis=1,
            tiled=True,
        ),
    )
    grad_gated = settled[0][0]
    grad_filter = settled[1][0]
    grad_value = key_values * grad_gated
    next_rim = from_behind(grad_value[:2], "seq", -1)
    longer = jnp.concatenate([grad_value, next_rim], axis=0)
    weights = short_weights[0]
    grad_input = (
        weights[0] * longer[:tok_rows]
        + weights[1] * longer[1 : tok_rows + 1]
        + weights[2] * longer[2:]
    )
    passed = shifted(grad_input.astype(jnp.bfloat16)[None], "pipe", -1)
    return (passed, grad_filter[None])


LANES = 128
RIM = 16
PARTS = 2
SPLIT = 4
MESH = pl.DeviceIdType.MESH


def half_step_tables(tokens, devices):
    half = tokens // 2
    odd = 2 * np.arange(half, dtype=np.int64)[:, None] + 1
    turns = (odd * np.arange(tokens, dtype=np.int64)[None, :]) % (4 * tokens)
    angles = turns * (2.0 * np.pi / (4 * tokens))
    part = half // PARTS
    share = tokens // devices // 2
    forward, inverse = [], []
    for parity in range(2):
        cosines, sines = np.cos(angles[:, parity::2]), np.sin(angles[:, parity::2])
        for first in range(0, half, part):
            forward.append(pair(np.concatenate([cosines[first : first + part], sines[first : first + part]])))
        back = np.concatenate([cosines, sines]).T
        back = np.concatenate([back, np.zeros((RIM, 2 * half))])
        for first in range(0, half, share):
            inverse.append(pair(back[first : first + share + RIM]))
    return (
        np.stack(forward).reshape(2, PARTS, 4 * part, half),
        np.stack(inverse).reshape(2, devices, 2 * (share + RIM), 2 * half),
    )


def pair(table):
    high = table.astype(jnp.bfloat16)
    low = (table - high.astype(np.float64)).astype(jnp.bfloat16)
    return np.concatenate([high, low])


def relay_kernel(
    devices, go_hbm, vb_hbm, kg_hbm, qg_hbm, sw, lf, fwd_hbm, inv_hbm,
    passed, fold_out,
    go, vb, kg, qg,
    conv_src, gated_src, both_all, gated_all, fwd, inv, mixed, woven,
    spec_both, spec_gated, packed, back_src, fold_src, back_got, fold_got, key_got, weight_got,
    load_sem, own_sem, send_sem, recv_sem, back_send, back_recv, side_send, side_recv,
):
    rows = go.shape[0]
    tokens = rows * devices
    half = tokens // 2
    share = rows // 2
    pipe = lax.axis_index("pipe")
    me = lax.axis_index("seq")
    other = 1 - pipe
    far_first = sorted(range(1, devices), key=lambda d: (abs(2 * d - devices), d))

    def gate(left, right, target):
        for block in range(devices):
            columns = pl.ds(block * LANES, LANES)
            value = left[:, columns].astype(jnp.float32) * right[:, columns].astype(jnp.float32)
            target[block] = value.astype(jnp.bfloat16)

    def peer(distance):
        return lax.rem(me + distance, devices)

    def behind(distance):
        return lax.rem(me + devices - distance, devices)

    barrier = pltpu.get_barrier_semaphore()
    for distance in range(devices):
        if distance:
            pl.semaphore_signal(
                barrier, inc=1, device_id={"pipe": pipe, "seq": peer(distance)}, device_id_type=MESH
            )
        pl.semaphore_signal(
            barrier, inc=1, device_id={"pipe": other, "seq": peer(distance)}, device_id_type=MESH
        )
    loads = []
    for i, (source, target) in enumerate(
        ((go_hbm.at[0], go), (qg_hbm.at[0], qg), (kg_hbm.at[0], kg), (vb_hbm.at[0], vb), (fwd_hbm, fwd), (inv_hbm, inv))
    ):
        copy = pltpu.make_async_copy(source, target, load_sem.at[i])
        loads.append(copy)
    for copy in loads[:4]:
        copy.start()
    pl.semaphore_wait(barrier, 2 * devices - 1)

    def lanes_of(device):
        return pl.ds(pl.multiple_of(device * LANES, LANES), LANES)

    def rows_of(device):
        return pl.ds(pl.multiple_of(device * rows, rows), rows)

    first, second = pl.ds(0, LANES), pl.ds(LANES, LANES)

    def scatter(kind, pick, target, columns):
        copies = []
        for distance in far_first:
            copy = pltpu.make_async_remote_copy(
                src_ref=pick(peer(distance)),
                dst_ref=target.at[rows_of(me), columns],
                send_sem=send_sem.at[kind, distance],
                recv_sem=recv_sem.at[kind, distance],
                device_id={"pipe": pipe, "seq": peer(distance)},
                device_id_type=MESH,
            )
            copy.start()
            copies.append(copy)
        own = pltpu.make_async_copy(
            pick(me), target.at[rows_of(me), columns], own_sem.at[kind]
        )
        own.start()
        return own, copies

    def landed(group):
        own, copies = group
        own.wait()
        for copy in copies:
            copy.wait_recv()

    filt_group = scatter(0, lambda device: lf.at[0, :, lanes_of(device)], both_all, first)
    loads[0].wait()
    loads[1].wait()
    gate(qg, go, conv_src)
    conv_group = scatter(1, lambda device: conv_src.at[device], both_all, second)
    for copy in loads[4:]:
        copy.start()
    loads[2].wait()
    loads[3].wait()
    gate(kg, vb, gated_src)
    side = []
    for i, (source, target, at) in enumerate(
        (
            (kg, key_got.at[pl.ds(0, rows)], me),
            (kg.at[pl.ds(0, RIM)], key_got.at[pl.ds(rows, RIM)], behind(1)),
            (sw, weight_got, me),
        )
    ):
        copy = pltpu.make_async_remote_copy(
            src_ref=source, dst_ref=target, send_sem=side_send.at[i], recv_sem=side_recv.at[i],
            device_id={"pipe": other, "seq": at}, device_id_type=MESH,
        )
        copy.start()
        side.append(copy)

    gated_group = scatter(2, lambda device: gated_src.at[device], gated_all, first)
    part = half // PARTS

    def transform(signal, target):
        width = signal.shape[1]
        evens, odds = [], []
        for at in range(0, width, LANES):
            mixed[...] = signal[:, pl.ds(at, LANES)].astype(jnp.float32)
            evens.append(mixed[pl.ds(0, half, stride=2), :].astype(jnp.bfloat16))
            odds.append(mixed[pl.ds(1, half, stride=2), :].astype(jnp.bfloat16))
        evens, odds = jnp.concatenate(evens, axis=1), jnp.concatenate(odds, axis=1)
        for i in range(PARTS):
            even = jnp.dot(fwd[0, i], evens, preferred_element_type=jnp.float32)
            even = even[: 2 * part] + even[2 * part :]
            odd = jnp.dot(fwd[1, i], odds, preferred_element_type=jnp.float32)
            odd = odd[: 2 * part] + odd[2 * part :]
            at = pl.ds(i * part, part)
            target[0, at, :] = even[:part] + odd[:part]
            target[1, at, :] = even[:part] - odd[:part]
            target[2, at, :] = odd[part:] + even[part:]
            target[3, at, :] = odd[part:] - even[part:]

    def pack(kind, parity, at, value):
        high = value.astype(jnp.bfloat16)
        packed[kind, parity, at, first] = high
        packed[kind, parity, at, second] = (value - high.astype(jnp.float32)).astype(jnp.bfloat16)

    def multiply(kind, spec_other):
        chunk = 64

        @pl.loop(0, half // chunk)
        def _(step):
            at = pl.ds(pl.multiple_of(step * chunk, chunk), chunk)
            low = pl.ds(pl.multiple_of(half + step * chunk, chunk), chunk)
            scale = 1.0 / tokens
            alike, cross = [], []
            for mirror in range(2):
                conv_cos = spec_both[mirror, at, second] * scale
                conv_sin = spec_both[2 + mirror, at, second] * scale
                other_cos, other_sin = spec_other[mirror, at, first], spec_other[2 + mirror, at, first]
                alike.append(conv_cos * other_cos + conv_sin * other_sin)
                cross.append(conv_sin * other_cos - conv_cos * other_sin)
            pack(kind, 0, at, alike[0] + alike[1])
            pack(kind, 0, low, cross[0] - cross[1])
            pack(kind, 1, at, alike[0] - alike[1])
            pack(kind, 1, low, cross[0] + cross[1])

    def invert(kind, block):
        for parity in range(2):
            wide = jnp.dot(inv[parity, block], packed[kind, parity], preferred_element_type=jnp.float32)
            wide = wide[: share + RIM] + wide[share + RIM :]
            wide = wide[:, :LANES] + wide[:, LANES:]
            woven[pl.ds(parity, share + RIM, stride=2), :] = wide

    def send_back(distance):
        invert(0, peer(distance))
        back_src[distance] = woven[pl.ds(0, rows + RIM), :].astype(jnp.bfloat16)
        copy = pltpu.make_async_remote_copy(
            src_ref=back_src.at[distance],
            dst_ref=back_got.at[me],
            send_sem=back_send.at[distance],
            recv_sem=back_recv.at[distance],
            device_id={"pipe": other, "seq": peer(distance)},
            device_id_type=MESH,
        )
        copy.start()
        return copy

    def send_fold(distance):
        invert(1, peer(distance))
        fold_src[distance] = woven[pl.ds(0, rows), :].astype(jnp.bfloat16)
        copy = pltpu.make_async_remote_copy(
            src_ref=fold_src.at[distance],
            dst_ref=fold_got.at[me],
            send_sem=send_sem.at[3, distance],
            recv_sem=recv_sem.at[3, distance],
            device_id={"pipe": pipe, "seq": peer(distance)},
            device_id_type=MESH,
        )
        copy.start()
        return copy

    loads[4].wait()
    landed(filt_group)
    landed(conv_group)
    transform(both_all, spec_both)
    multiply(0, spec_both)
    loads[5].wait()
    backs = [send_back(distance) for distance in far_first]
    landed(gated_group)
    transform(gated_all, spec_gated)
    multiply(1, spec_gated)
    folds = [send_fold(distance) for distance in far_first]
    backs.append(send_back(0))
    invert(1, me)
    fold_out[0, :, lanes_of(me)] = woven[pl.ds(0, rows), :]

    for copy in side:
        copy.wait_recv()
    for copy, distance in zip(backs, far_first + [0]):
        copy.wait_recv()
        columns = lanes_of(behind(distance))
        value = key_got[:, columns].astype(jnp.float32) * back_got[behind(distance)].astype(jnp.float32)
        extent = rows + RIM
        total = weight_got[0, :, columns] * value
        total += weight_got[1, :, columns] * pltpu.roll(value, extent - 1, 0)
        total += weight_got[2, :, columns] * pltpu.roll(value, extent - 2, 0)
        passed[0, :, columns] = total[:rows].astype(jnp.bfloat16)
    for copy, distance in zip(folds, far_first):
        copy.wait_recv()
        fold_out[0, :, lanes_of(behind(distance))] = fold_got[behind(distance)].astype(jnp.float32)
    for copy in filt_group[1] + conv_group[1] + gated_group[1] + side + backs + folds:
        copy.wait_send()


def relay_body(grad_out, value_branch, key_gate, query_gate, short_weights, long_filters):
    _, rows, columns = grad_out.shape
    devices = lax.axis_size("seq")
    tokens = rows * devices
    tables = [jnp.asarray(table) for table in half_step_tables(tokens, devices)]
    vmem = pl.BlockSpec(memory_space=pltpu.VMEM)
    anywhere = pl.BlockSpec(memory_space=pltpu.HBM)
    half, full = jnp.bfloat16, jnp.float32
    passed, fold = pl.pallas_call(
        functools.partial(relay_kernel, devices),
        out_shape=(
            pltpu.VMEM((1, rows, columns), half),
            pltpu.VMEM((1, rows, columns), full),
        ),
        in_specs=[anywhere] * 8,
        out_specs=(vmem, vmem),
        scratch_shapes=[pltpu.VMEM((rows, columns), half)] * 4
        + [pltpu.VMEM((devices, rows, LANES), half)] * 2
        + [
            pltpu.VMEM((tokens, 2 * LANES), half),
            pltpu.VMEM((tokens, LANES), half),
            pltpu.VMEM(tables[0].shape, half),
            pltpu.VMEM(tables[1].shape, half),
            pltpu.VMEM((tokens, LANES), full),
            pltpu.VMEM((rows + 2 * RIM, LANES), full),
            pltpu.VMEM((4, tokens // 2, 2 * LANES), full),
            pltpu.VMEM((4, tokens // 2, LANES), full),
            pltpu.VMEM((2, 2, tokens, 2 * LANES), half),
            pltpu.VMEM((devices, rows + RIM, LANES), half),
            pltpu.VMEM((devices, rows, LANES), half),
            pltpu.VMEM((devices, rows + RIM, LANES), half),
            pltpu.VMEM((devices, rows, LANES), half),
            pltpu.VMEM((rows + RIM, columns), half),
            pltpu.VMEM((3, 1, columns), full),
            pltpu.SemaphoreType.DMA((6,)),
            pltpu.SemaphoreType.DMA((3,)),
            pltpu.SemaphoreType.DMA((4, devices)),
            pltpu.SemaphoreType.DMA((4, devices)),
            pltpu.SemaphoreType.DMA((devices,)),
            pltpu.SemaphoreType.DMA((devices,)),
            pltpu.SemaphoreType.DMA((3,)),
            pltpu.SemaphoreType.DMA((3,)),
        ],
        compiler_params=pltpu.CompilerParams(
            collective_id=0, has_side_effects=True, vmem_limit_bytes=62 * 2**20
        ),
        cost_estimate=pl.CostEstimate(
            flops=16 * tokens * tokens * LANES, bytes_accessed=10 * tokens * tokens, transcendentals=0
        ),
    )(
        grad_out, value_branch, key_gate, query_gate,
        jnp.transpose(short_weights, (1, 0, 2)), long_filters, *tables,
    )
    return pl.pallas_call(
        settle_kernel,
        out_shape=(
            jax.ShapeDtypeStruct(passed.shape, half),
            jax.ShapeDtypeStruct(fold.shape, full),
        ),
        in_specs=[vmem, vmem],
        out_specs=(anywhere, anywhere),
        scratch_shapes=[pltpu.SemaphoreType.DMA((2, SPLIT))],
        compiler_params=pltpu.CompilerParams(vmem_limit_bytes=16 * 2**20),
    )(passed, fold)


def settle_kernel(passed, fold, passed_out, fold_out, sem):
    copies = []
    for i, (source, target) in enumerate(((fold, fold_out), (passed, passed_out))):
        step = source.shape[1] // SPLIT
        for j in range(SPLIT):
            at = pl.ds(j * step, step)
            copies.append(pltpu.make_async_copy(source.at[:, at], target.at[:, at], sem.at[i, j]))
    for copy in copies:
        copy.start()
    for copy in copies:
        copy.wait()


def solution(mesh):
    placed = (
        P("pipe", "seq", "chan"),
        P("pipe", "seq", "chan"),
        P("pipe", "seq", "chan"),
        P("pipe", "seq", "chan"),
        P("pipe", None, "chan"),
        P("pipe", "seq", "chan"),
    )

    def run(*arrays):
        _, tokens, channels = arrays[0].shape
        devices = mesh.shape["seq"]
        fits = (
            mesh.shape["pipe"] == 2
            and devices > 1
            and channels == mesh.shape["chan"] * devices * LANES
            and tokens <= 1024
            and tokens % (2 * devices * RIM) == 0
            and tokens % (2 * LANES) == 0
        )
        return jax.shard_map(
            relay_body if fits else spread_body,
            mesh=mesh,
            in_specs=placed,
            out_specs=(P("pipe", "seq", "chan"), P("pipe", "seq", "chan")),
            check_vma=False,
        )(*arrays)

    return run
```

```python
import functools
import math

import jax
import jax.numpy as jnp
import numpy as np
from jax import lax
from jax.experimental import pallas as pl
from jax.experimental.pallas import tpu as pltpu
from jax.sharding import PartitionSpec as P


def from_behind(value, axis, by):
    devices = lax.axis_size(axis)
    pairs = [(i, i + by) for i in range(devices) if 0 <= i + by < devices]
    return lax.ppermute(value, axis, pairs)


def shifted(block, axis, distance):
    devices = range(lax.axis_size(axis))
    route = [((i - distance) % len(devices), i) for i in devices]
    return lax.ppermute(block, axis, route)


def phase_table(product, modulus):
    angles = (product % modulus).astype(jnp.float32) * (2.0 * math.pi / modulus)
    return (jnp.cos(angles), jnp.sin(angles))


def contract(form, table, values):
    return jnp.einsum(form, table, values, precision=lax.Precision.HIGHEST)


def forward_blocks(signal, row_first, padded):
    block_count = signal.shape[0]
    row_count = signal.shape[1]
    frequency = jnp.arange(2 * block_count, dtype=jnp.int32)
    block_index = jnp.arange(block_count, dtype=jnp.int32)
    cos_table, sin_table = phase_table(frequency[:, None] * block_index[None, :], 2 * block_count)
    real_part = contract("ca,arx->crx", cos_table, signal)
    imag_part = -contract("ca,arx->crx", sin_table, signal)
    row_index = row_first + jnp.arange(row_count, dtype=jnp.int32)
    cos_twist, sin_twist = phase_table(frequency[:, None] * row_index[None, :], padded)
    cos_twist = cos_twist[:, :, None]
    sin_twist = sin_twist[:, :, None]
    return (
        real_part * cos_twist + imag_part * sin_twist,
        imag_part * cos_twist - real_part * sin_twist,
    )


def along_rows(real_part, imag_part, direction):
    length = real_part.shape[1]
    indices = jnp.arange(length, dtype=jnp.int32)
    cos_table, sin_table = phase_table(indices[:, None] * indices[None, :], length)
    cos_real = contract("dr,crx->cdx", cos_table, real_part)
    cos_imag = contract("dr,crx->cdx", cos_table, imag_part)
    sin_real = contract("dr,crx->cdx", sin_table, real_part)
    sin_imag = contract("dr,crx->cdx", sin_table, imag_part)
    return (cos_real - direction * sin_imag, cos_imag + direction * sin_real)


def inverse_twist(real_part, imag_part, freq_first, padded):
    frequency = freq_first + jnp.arange(real_part.shape[0], dtype=jnp.int32)
    row_index = jnp.arange(real_part.shape[1], dtype=jnp.int32)
    cos_twist, sin_twist = phase_table(frequency[:, None] * row_index[None, :], padded)
    cos_twist = cos_twist[:, :, None]
    sin_twist = sin_twist[:, :, None]
    return (
        real_part * cos_twist - imag_part * sin_twist,
        imag_part * cos_twist + real_part * sin_twist,
    )


def inverse_blocks(real_part, imag_part, padded):
    block_count = real_part.shape[0] // 2
    block_index = jnp.arange(block_count, dtype=jnp.int32)
    frequency = jnp.arange(2 * block_count, dtype=jnp.int32)
    cos_table, sin_table = phase_table(block_index[:, None] * frequency[None, :], 2 * block_count)
    summed = contract("ac,crx->arx", cos_table, real_part) - contract(
        "ac,crx->arx", sin_table, imag_part
    )
    return summed * (1.0 / padded)


def spectral_products(conv_real, conv_imag, gated_real, gated_imag, filter_real, filter_imag):
    back_real = conv_real * filter_real + conv_imag * filter_imag
    back_imag = conv_imag * filter_real - conv_real * filter_imag
    fold_real = conv_real * gated_real + conv_imag * gated_imag
    fold_imag = conv_imag * gated_real - conv_real * gated_imag
    return (back_real, back_imag, fold_real, fold_imag)


def spread_body(grad_out, value_branch, key_gate, query_gate, short_weights, long_filters):
    grad_y = grad_out[0]
    tok_rows, columns = grad_y.shape
    devices = lax.axis_size("seq")
    position = lax.axis_index("seq")
    padded = 2 * tok_rows * devices
    key_values = key_gate[0].astype(jnp.float32)
    grad_conv = (query_gate[0].astype(jnp.float32) * grad_y.astype(jnp.float32)).astype(
        jnp.bfloat16
    )
    gated_value = (key_values * value_branch[0].astype(jnp.float32)).astype(jnp.bfloat16)
    per_device = tok_rows // devices
    pieces = (
        lax.all_to_all(grad_conv[None], "seq", split_axis=1, concat_axis=0, tiled=True),
        lax.all_to_all(gated_value[None], "seq", split_axis=1, concat_axis=0, tiled=True),
        lax.all_to_all(long_filters, "seq", split_axis=1, concat_axis=0, tiled=True),
    )
    halves = [
        forward_blocks(piece.astype(jnp.float32), position * per_device, padded) for piece in pieces
    ]
    exchanged = (
        lax.all_to_all(halves[0][0], "seq", split_axis=0, concat_axis=1, tiled=True),
        lax.all_to_all(halves[0][1], "seq", split_axis=0, concat_axis=1, tiled=True),
        lax.all_to_all(halves[1][0], "seq", split_axis=0, concat_axis=1, tiled=True),
        lax.all_to_all(halves[1][1], "seq", split_axis=0, concat_axis=1, tiled=True),
        lax.all_to_all(halves[2][0], "seq", split_axis=0, concat_axis=1, tiled=True),
        lax.all_to_all(halves[2][1], "seq", split_axis=0, concat_axis=1, tiled=True),
    )
    conv_real, conv_imag = along_rows(exchanged[0], exchanged[1], -1.0)
    gated_real, gated_imag = along_rows(exchanged[2], exchanged[3], -1.0)
    filter_real, filter_imag = along_rows(exchanged[4], exchanged[5], -1.0)
    back_real, back_imag, fold_real, fold_imag = spectral_products(
        conv_real, conv_imag, gated_real, gated_imag, filter_real, filter_imag
    )
    pair_count = fold_real.shape[0]
    back_real, back_imag = along_rows(back_real, back_imag, 1.0)
    back_real, back_imag = inverse_twist(back_real, back_imag, position * pair_count, padded)
    fold_real, fold_imag = along_rows(fold_real, fold_imag, 1.0)
    fold_real, fold_imag = inverse_twist(fold_real, fold_imag, position * pair_count, padded)
    returned = (
        lax.all_to_all(back_real, "seq", split_axis=1, concat_axis=0, tiled=True),
        lax.all_to_all(back_imag, "seq", split_axis=1, concat_axis=0, tiled=True),
        lax.all_to_all(fold_real, "seq", split_axis=1, concat_axis=0, tiled=True),
        lax.all_to_all(fold_imag, "seq", split_axis=1, concat_axis=0, tiled=True),
    )
    settled = (
        lax.all_to_all(
            inverse_blocks(returned[0], returned[1], padded),
            "seq",
            split_axis=0,
            concat_axis=1,
            tiled=True,
        ),
        lax.all_to_all(
            inverse_blocks(returned[2], returned[3], padded),
            "seq",
            split_axis=0,
            concat_axis=1,
            tiled=True,
        ),
    )
    grad_gated = settled[0][0]
    grad_filter = settled[1][0]
    grad_value = key_values * grad_gated
    next_rim = from_behind(grad_value[:2], "seq", -1)
    longer = jnp.concatenate([grad_value, next_rim], axis=0)
    weights = short_weights[0]
    grad_input = (
        weights[0] * longer[:tok_rows]
        + weights[1] * longer[1 : tok_rows + 1]
        + weights[2] * longer[2:]
    )
    passed = shifted(grad_input.astype(jnp.bfloat16)[None], "pipe", -1)
    return (passed, grad_filter[None])


LANES = 128
RIM = 16
PARTS = 2
SPLIT = 4
MESH = pl.DeviceIdType.MESH


def half_step_tables(tokens, devices):
    half = tokens // 2
    odd = 2 * np.arange(half, dtype=np.int64)[:, None] + 1
    turns = (odd * np.arange(tokens, dtype=np.int64)[None, :]) % (4 * tokens)
    angles = turns * (2.0 * np.pi / (4 * tokens))
    part = half // PARTS
    share = tokens // devices // 2
    forward, inverse = [], []
    for parity in range(2):
        cosines, sines = np.cos(angles[:, parity::2]), np.sin(angles[:, parity::2])
        for first in range(0, half, part):
            forward.append(pair(np.concatenate([cosines[first : first + part], sines[first : first + part]])))
        back = np.concatenate([cosines, sines]).T
        back = np.concatenate([back, np.zeros((RIM, 2 * half))])
        for first in range(0, half, share):
            inverse.append(pair(back[first : first + share + RIM]))
    return (
        np.stack(forward).reshape(2, PARTS, 4 * part, half),
        np.stack(inverse).reshape(2, devices, 2 * (share + RIM), 2 * half),
    )


def pair(table):
    high = table.astype(jnp.bfloat16)
    low = (table - high.astype(np.float64)).astype(jnp.bfloat16)
    return np.concatenate([high, low])


def relay_kernel(
    devices, go_hbm, vb_hbm, kg_hbm, qg_hbm, sw, lf, fwd_hbm, inv_hbm,
    passed, fold_out,
    go, vb, kg, qg,
    conv_src, gated_src, both_all, gated_all, fwd, inv, mixed, woven,
    spec_both, spec_gated, packed, back_src, fold_src, back_got, fold_got, key_got, weight_got,
    load_sem, own_sem, send_sem, recv_sem, back_send, back_recv, side_send, side_recv, late_sem,
):
    rows = go.shape[0]
    tokens = rows * devices
    half = tokens // 2
    share = rows // 2
    pipe = lax.axis_index("pipe")
    me = lax.axis_index("seq")
    other = 1 - pipe
    far_first = sorted(range(1, devices), key=lambda d: (abs(2 * d - devices), d))

    def gate(left, right, target):
        for block in range(devices):
            columns = pl.ds(block * LANES, LANES)
            value = left[:, columns].astype(jnp.float32) * right[:, columns].astype(jnp.float32)
            target[block] = value.astype(jnp.bfloat16)

    def peer(distance):
        return lax.rem(me + distance, devices)

    def behind(distance):
        return lax.rem(me + devices - distance, devices)

    last = devices - 1
    late = me == last

    def slot_peer(slot):
        early = lax.rem(me + 1 + slot, last) if slot < last - 1 else last
        return jnp.where(late, slot, early)

    def greet(semaphore, device_pipe, at):
        pl.semaphore_signal(
            semaphore, inc=1, device_id={"pipe": device_pipe, "seq": at}, device_id_type=MESH
        )

    barrier = pltpu.get_barrier_semaphore()
    greet(barrier, other, me)

    @pl.when(jnp.logical_not(late))
    def _():
        for slot in range(last):
            greet(barrier, pipe, slot_peer(slot))
            greet(barrier, other, slot_peer(slot))

    loads = []
    for i, (source, target) in enumerate(
        ((go_hbm.at[0], go), (qg_hbm.at[0], qg), (kg_hbm.at[0], kg), (vb_hbm.at[0], vb), (fwd_hbm, fwd), (inv_hbm, inv))
    ):
        copy = pltpu.make_async_copy(source, target, load_sem.at[i])
        loads.append(copy)
    for copy in loads[:4]:
        copy.start()
    pl.semaphore_wait(barrier, jnp.where(late, 2 * devices - 1, 2 * last - 1))

    @pl.when(late)
    def _():
        for slot in range(last):
            greet(late_sem, pipe, slot_peer(slot))
            greet(late_sem, other, slot_peer(slot))

    def lanes_of(device):
        return pl.ds(pl.multiple_of(device * LANES, LANES), LANES)

    def rows_of(device):
        return pl.ds(pl.multiple_of(device * rows, rows), rows)

    first, second = pl.ds(0, LANES), pl.ds(LANES, LANES)

    def scatter(kind, pick, target, columns):
        sends, arrivals = [], []
        for slot in range(last):
            at = slot_peer(slot)
            for index, copies in ((me, sends), (at, arrivals)):
                copies.append(
                    pltpu.make_async_remote_copy(
                        src_ref=pick(at),
                        dst_ref=target.at[rows_of(index), columns],
                        send_sem=send_sem.at[kind, slot],
                        recv_sem=recv_sem.at[kind, index],
                        device_id={"pipe": pipe, "seq": at},
                        device_id_type=MESH,
                    )
                )
        for copy in sends[:-1]:
            copy.start()
        own = pltpu.make_async_copy(
            pick(me), target.at[rows_of(me), columns], own_sem.at[kind]
        )
        own.start()
        return own, sends, arrivals

    def landed(group):
        own, _, arrivals = group
        own.wait()
        for copy in arrivals:
            copy.wait_recv()

    filt_group = scatter(0, lambda device: lf.at[0, :, lanes_of(device)], both_all, first)
    loads[0].wait()
    loads[1].wait()
    gate(qg, go, conv_src)
    conv_group = scatter(1, lambda device: conv_src.at[device], both_all, second)

    @pl.when(jnp.logical_not(late))
    def _():
        pl.semaphore_wait(late_sem, 2)

    filt_group[1][-1].start()
    conv_group[1][-1].start()
    for copy in loads[4:]:
        copy.start()
    loads[2].wait()
    loads[3].wait()
    gate(kg, vb, gated_src)
    side = []
    for i, (source, target, at) in enumerate(
        (
            (kg, key_got.at[pl.ds(0, rows)], me),
            (kg.at[pl.ds(0, RIM)], key_got.at[pl.ds(rows, RIM)], behind(1)),
            (sw, weight_got, me),
        )
    ):
        copy = pltpu.make_async_remote_copy(
            src_ref=source, dst_ref=target, send_sem=side_send.at[i], recv_sem=side_recv.at[i],
            device_id={"pipe": other, "seq": at}, device_id_type=MESH,
        )
        copy.start()
        side.append(copy)

    gated_group = scatter(2, lambda device: gated_src.at[device], gated_all, first)
    gated_group[1][-1].start()
    part = half // PARTS

    def transform(signal, target):
        width = signal.shape[1]
        evens, odds = [], []
        for at in range(0, width, LANES):
            mixed[...] = signal[:, pl.ds(at, LANES)].astype(jnp.float32)
            evens.append(mixed[pl.ds(0, half, stride=2), :].astype(jnp.bfloat16))
            odds.append(mixed[pl.ds(1, half, stride=2), :].astype(jnp.bfloat16))
        evens, odds = jnp.concatenate(evens, axis=1), jnp.concatenate(odds, axis=1)
        for i in range(PARTS):
            even = jnp.dot(fwd[0, i], evens, preferred_element_type=jnp.float32)
            even = even[: 2 * part] + even[2 * part :]
            odd = jnp.dot(fwd[1, i], odds, preferred_element_type=jnp.float32)
            odd = odd[: 2 * part] + odd[2 * part :]
            at = pl.ds(i * part, part)
            target[0, at, :] = even[:part] + odd[:part]
            target[1, at, :] = even[:part] - odd[:part]
            target[2, at, :] = odd[part:] + even[part:]
            target[3, at, :] = odd[part:] - even[part:]

    def pack(kind, parity, at, value):
        high = value.astype(jnp.bfloat16)
        packed[kind, parity, at, first] = high
        packed[kind, parity, at, second] = (value - high.astype(jnp.float32)).astype(jnp.bfloat16)

    def multiply(kind, spec_other):
        chunk = 64

        @pl.loop(0, half // chunk)
        def _(step):
            at = pl.ds(pl.multiple_of(step * chunk, chunk), chunk)
            low = pl.ds(pl.multiple_of(half + step * chunk, chunk), chunk)
            scale = 1.0 / tokens
            alike, cross = [], []
            for mirror in range(2):
                conv_cos = spec_both[mirror, at, second] * scale
                conv_sin = spec_both[2 + mirror, at, second] * scale
                other_cos, other_sin = spec_other[mirror, at, first], spec_other[2 + mirror, at, first]
                alike.append(conv_cos * other_cos + conv_sin * other_sin)
                cross.append(conv_sin * other_cos - conv_cos * other_sin)
            pack(kind, 0, at, alike[0] + alike[1])
            pack(kind, 0, low, cross[0] - cross[1])
            pack(kind, 1, at, alike[0] - alike[1])
            pack(kind, 1, low, cross[0] + cross[1])

    def invert(kind, block):
        for parity in range(2):
            wide = jnp.dot(inv[parity, block], packed[kind, parity], preferred_element_type=jnp.float32)
            wide = wide[: share + RIM] + wide[share + RIM :]
            wide = wide[:, :LANES] + wide[:, LANES:]
            woven[pl.ds(parity, share + RIM, stride=2), :] = wide

    def send_back(distance):
        invert(0, peer(distance))
        back_src[distance] = woven[pl.ds(0, rows + RIM), :].astype(jnp.bfloat16)
        copy = pltpu.make_async_remote_copy(
            src_ref=back_src.at[distance],
            dst_ref=back_got.at[me],
            send_sem=back_send.at[distance],
            recv_sem=back_recv.at[distance],
            device_id={"pipe": other, "seq": peer(distance)},
            device_id_type=MESH,
        )
        copy.start()
        return copy

    def send_fold(distance):
        invert(1, peer(distance))
        fold_src[distance] = woven[pl.ds(0, rows), :].astype(jnp.bfloat16)
        copy = pltpu.make_async_remote_copy(
            src_ref=fold_src.at[distance],
            dst_ref=fold_got.at[me],
            send_sem=send_sem.at[3, distance],
            recv_sem=recv_sem.at[3, distance],
            device_id={"pipe": pipe, "seq": peer(distance)},
            device_id_type=MESH,
        )
        copy.start()
        return copy

    loads[4].wait()
    landed(filt_group)
    landed(conv_group)
    transform(both_all, spec_both)
    multiply(0, spec_both)
    loads[5].wait()
    backs = [send_back(distance) for distance in far_first]
    landed(gated_group)
    transform(gated_all, spec_gated)
    multiply(1, spec_gated)
    folds = [send_fold(distance) for distance in far_first]
    backs.append(send_back(0))
    invert(1, me)
    fold_out[0, :, lanes_of(me)] = woven[pl.ds(0, rows), :]

    for copy in side:
        copy.wait_recv()
    for copy, distance in zip(backs, far_first + [0]):
        copy.wait_recv()
        columns = lanes_of(behind(distance))
        value = key_got[:, columns].astype(jnp.float32) * back_got[behind(distance)].astype(jnp.float32)
        extent = rows + RIM
        total = weight_got[0, :, columns] * value
        total += weight_got[1, :, columns] * pltpu.roll(value, extent - 1, 0)
        total += weight_got[2, :, columns] * pltpu.roll(value, extent - 2, 0)
        passed[0, :, columns] = total[:rows].astype(jnp.bfloat16)
    for copy, distance in zip(folds, far_first):
        copy.wait_recv()
        fold_out[0, :, lanes_of(behind(distance))] = fold_got[behind(distance)].astype(jnp.float32)
    for copy in filt_group[1] + conv_group[1] + gated_group[1] + side + backs + folds:
        copy.wait_send()


def relay_body(grad_out, value_branch, key_gate, query_gate, short_weights, long_filters):
    _, rows, columns = grad_out.shape
    devices = lax.axis_size("seq")
    tokens = rows * devices
    tables = [jnp.asarray(table) for table in half_step_tables(tokens, devices)]
    vmem = pl.BlockSpec(memory_space=pltpu.VMEM)
    anywhere = pl.BlockSpec(memory_space=pltpu.HBM)
    half, full = jnp.bfloat16, jnp.float32
    passed, fold = pl.pallas_call(
        functools.partial(relay_kernel, devices),
        out_shape=(
            pltpu.VMEM((1, rows, columns), half),
            pltpu.VMEM((1, rows, columns), full),
        ),
        in_specs=[anywhere] * 8,
        out_specs=(vmem, vmem),
        scratch_shapes=[pltpu.VMEM((rows, columns), half)] * 4
        + [pltpu.VMEM((devices, rows, LANES), half)] * 2
        + [
            pltpu.VMEM((tokens, 2 * LANES), half),
            pltpu.VMEM((tokens, LANES), half),
            pltpu.VMEM(tables[0].shape, half),
            pltpu.VMEM(tables[1].shape, half),
            pltpu.VMEM((tokens, LANES), full),
            pltpu.VMEM((rows + 2 * RIM, LANES), full),
            pltpu.VMEM((4, tokens // 2, 2 * LANES), full),
            pltpu.VMEM((4, tokens // 2, LANES), full),
            pltpu.VMEM((2, 2, tokens, 2 * LANES), half),
            pltpu.VMEM((devices, rows + RIM, LANES), half),
            pltpu.VMEM((devices, rows, LANES), half),
            pltpu.VMEM((devices, rows + RIM, LANES), half),
            pltpu.VMEM((devices, rows, LANES), half),
            pltpu.VMEM((rows + RIM, columns), half),
            pltpu.VMEM((3, 1, columns), full),
            pltpu.SemaphoreType.DMA((6,)),
            pltpu.SemaphoreType.DMA((3,)),
            pltpu.SemaphoreType.DMA((4, devices)),
            pltpu.SemaphoreType.DMA((4, devices)),
            pltpu.SemaphoreType.DMA((devices,)),
            pltpu.SemaphoreType.DMA((devices,)),
            pltpu.SemaphoreType.DMA((3,)),
            pltpu.SemaphoreType.DMA((3,)),
            pltpu.SemaphoreType.REGULAR,
        ],
        compiler_params=pltpu.CompilerParams(
            collective_id=0, has_side_effects=True, vmem_limit_bytes=62 * 2**20
        ),
        cost_estimate=pl.CostEstimate(
            flops=16 * tokens * tokens * LANES, bytes_accessed=10 * tokens * tokens, transcendentals=0
        ),
    )(
        grad_out, value_branch, key_gate, query_gate,
        jnp.transpose(short_weights, (1, 0, 2)), long_filters, *tables,
    )
    return pl.pallas_call(
        settle_kernel,
        out_shape=(
            jax.ShapeDtypeStruct(passed.shape, half),
            jax.ShapeDtypeStruct(fold.shape, full),
        ),
        in_specs=[vmem, vmem],
        out_specs=(anywhere, anywhere),
        scratch_shapes=[pltpu.SemaphoreType.DMA((2, SPLIT))],
        compiler_params=pltpu.CompilerParams(vmem_limit_bytes=16 * 2**20),
    )(passed, fold)


def settle_kernel(passed, fold, passed_out, fold_out, sem):
    copies = []
    for i, (source, target) in enumerate(((fold, fold_out), (passed, passed_out))):
        step = source.shape[1] // SPLIT
        for j in range(SPLIT):
            at = pl.ds(j * step, step)
            copies.append(pltpu.make_async_copy(source.at[:, at], target.at[:, at], sem.at[i, j]))
    for copy in copies:
        copy.start()
    for copy in copies:
        copy.wait()


def solution(mesh):
    placed = (
        P("pipe", "seq", "chan"),
        P("pipe", "seq", "chan"),
        P("pipe", "seq", "chan"),
        P("pipe", "seq", "chan"),
        P("pipe", None, "chan"),
        P("pipe", "seq", "chan"),
    )

    def run(*arrays):
        _, tokens, channels = arrays[0].shape
        devices = mesh.shape["seq"]
        fits = (
            mesh.shape["pipe"] == 2
            and devices > 1
            and channels == mesh.shape["chan"] * devices * LANES
            and tokens <= 1024
            and tokens % (2 * devices * RIM) == 0
            and tokens % (2 * LANES) == 0
        )
        return jax.shard_map(
            relay_body if fits else spread_body,
            mesh=mesh,
            in_specs=placed,
            out_specs=(P("pipe", "seq", "chan"), P("pipe", "seq", "chan")),
            check_vma=False,
        )(*arrays)

    return run
```

```python
import functools
import math

import jax
import jax.numpy as jnp
import numpy as np
from jax import lax
from jax.experimental import pallas as pl
from jax.experimental.pallas import tpu as pltpu
from jax.sharding import PartitionSpec as P


def from_behind(value, axis, by):
    devices = lax.axis_size(axis)
    pairs = [(i, i + by) for i in range(devices) if 0 <= i + by < devices]
    return lax.ppermute(value, axis, pairs)


def shifted(block, axis, distance):
    devices = range(lax.axis_size(axis))
    route = [((i - distance) % len(devices), i) for i in devices]
    return lax.ppermute(block, axis, route)


def phase_table(product, modulus):
    angles = (product % modulus).astype(jnp.float32) * (2.0 * math.pi / modulus)
    return (jnp.cos(angles), jnp.sin(angles))


def contract(form, table, values):
    return jnp.einsum(form, table, values, precision=lax.Precision.HIGHEST)


def forward_blocks(signal, row_first, padded):
    block_count = signal.shape[0]
    row_count = signal.shape[1]
    frequency = jnp.arange(2 * block_count, dtype=jnp.int32)
    block_index = jnp.arange(block_count, dtype=jnp.int32)
    cos_table, sin_table = phase_table(frequency[:, None] * block_index[None, :], 2 * block_count)
    real_part = contract("ca,arx->crx", cos_table, signal)
    imag_part = -contract("ca,arx->crx", sin_table, signal)
    row_index = row_first + jnp.arange(row_count, dtype=jnp.int32)
    cos_twist, sin_twist = phase_table(frequency[:, None] * row_index[None, :], padded)
    cos_twist = cos_twist[:, :, None]
    sin_twist = sin_twist[:, :, None]
    return (
        real_part * cos_twist + imag_part * sin_twist,
        imag_part * cos_twist - real_part * sin_twist,
    )


def along_rows(real_part, imag_part, direction):
    length = real_part.shape[1]
    indices = jnp.arange(length, dtype=jnp.int32)
    cos_table, sin_table = phase_table(indices[:, None] * indices[None, :], length)
    cos_real = contract("dr,crx->cdx", cos_table, real_part)
    cos_imag = contract("dr,crx->cdx", cos_table, imag_part)
    sin_real = contract("dr,crx->cdx", sin_table, real_part)
    sin_imag = contract("dr,crx->cdx", sin_table, imag_part)
    return (cos_real - direction * sin_imag, cos_imag + direction * sin_real)


def inverse_twist(real_part, imag_part, freq_first, padded):
    frequency = freq_first + jnp.arange(real_part.shape[0], dtype=jnp.int32)
    row_index = jnp.arange(real_part.shape[1], dtype=jnp.int32)
    cos_twist, sin_twist = phase_table(frequency[:, None] * row_index[None, :], padded)
    cos_twist = cos_twist[:, :, None]
    sin_twist = sin_twist[:, :, None]
    return (
        real_part * cos_twist - imag_part * sin_twist,
        imag_part * cos_twist + real_part * sin_twist,
    )


def inverse_blocks(real_part, imag_part, padded):
    block_count = real_part.shape[0] // 2
    block_index = jnp.arange(block_count, dtype=jnp.int32)
    frequency = jnp.arange(2 * block_count, dtype=jnp.int32)
    cos_table, sin_table = phase_table(block_index[:, None] * frequency[None, :], 2 * block_count)
    summed = contract("ac,crx->arx", cos_table, real_part) - contract(
        "ac,crx->arx", sin_table, imag_part
    )
    return summed * (1.0 / padded)


def spectral_products(conv_real, conv_imag, gated_real, gated_imag, filter_real, filter_imag):
    back_real = conv_real * filter_real + conv_imag * filter_imag
    back_imag = conv_imag * filter_real - conv_real * filter_imag
    fold_real = conv_real * gated_real + conv_imag * gated_imag
    fold_imag = conv_imag * gated_real - conv_real * gated_imag
    return (back_real, back_imag, fold_real, fold_imag)


def spread_body(grad_out, value_branch, key_gate, query_gate, short_weights, long_filters):
    grad_y = grad_out[0]
    tok_rows, columns = grad_y.shape
    devices = lax.axis_size("seq")
    position = lax.axis_index("seq")
    padded = 2 * tok_rows * devices
    key_values = key_gate[0].astype(jnp.float32)
    grad_conv = (query_gate[0].astype(jnp.float32) * grad_y.astype(jnp.float32)).astype(
        jnp.bfloat16
    )
    gated_value = (key_values * value_branch[0].astype(jnp.float32)).astype(jnp.bfloat16)
    per_device = tok_rows // devices
    pieces = (
        lax.all_to_all(grad_conv[None], "seq", split_axis=1, concat_axis=0, tiled=True),
        lax.all_to_all(gated_value[None], "seq", split_axis=1, concat_axis=0, tiled=True),
        lax.all_to_all(long_filters, "seq", split_axis=1, concat_axis=0, tiled=True),
    )
    halves = [
        forward_blocks(piece.astype(jnp.float32), position * per_device, padded) for piece in pieces
    ]
    exchanged = (
        lax.all_to_all(halves[0][0], "seq", split_axis=0, concat_axis=1, tiled=True),
        lax.all_to_all(halves[0][1], "seq", split_axis=0, concat_axis=1, tiled=True),
        lax.all_to_all(halves[1][0], "seq", split_axis=0, concat_axis=1, tiled=True),
        lax.all_to_all(halves[1][1], "seq", split_axis=0, concat_axis=1, tiled=True),
        lax.all_to_all(halves[2][0], "seq", split_axis=0, concat_axis=1, tiled=True),
        lax.all_to_all(halves[2][1], "seq", split_axis=0, concat_axis=1, tiled=True),
    )
    conv_real, conv_imag = along_rows(exchanged[0], exchanged[1], -1.0)
    gated_real, gated_imag = along_rows(exchanged[2], exchanged[3], -1.0)
    filter_real, filter_imag = along_rows(exchanged[4], exchanged[5], -1.0)
    back_real, back_imag, fold_real, fold_imag = spectral_products(
        conv_real, conv_imag, gated_real, gated_imag, filter_real, filter_imag
    )
    pair_count = fold_real.shape[0]
    back_real, back_imag = along_rows(back_real, back_imag, 1.0)
    back_real, back_imag = inverse_twist(back_real, back_imag, position * pair_count, padded)
    fold_real, fold_imag = along_rows(fold_real, fold_imag, 1.0)
    fold_real, fold_imag = inverse_twist(fold_real, fold_imag, position * pair_count, padded)
    returned = (
        lax.all_to_all(back_real, "seq", split_axis=1, concat_axis=0, tiled=True),
        lax.all_to_all(back_imag, "seq", split_axis=1, concat_axis=0, tiled=True),
        lax.all_to_all(fold_real, "seq", split_axis=1, concat_axis=0, tiled=True),
        lax.all_to_all(fold_imag, "seq", split_axis=1, concat_axis=0, tiled=True),
    )
    settled = (
        lax.all_to_all(
            inverse_blocks(returned[0], returned[1], padded),
            "seq",
            split_axis=0,
            concat_axis=1,
            tiled=True,
        ),
        lax.all_to_all(
            inverse_blocks(returned[2], returned[3], padded),
            "seq",
            split_axis=0,
            concat_axis=1,
            tiled=True,
        ),
    )
    grad_gated = settled[0][0]
    grad_filter = settled[1][0]
    grad_value = key_values * grad_gated
    next_rim = from_behind(grad_value[:2], "seq", -1)
    longer = jnp.concatenate([grad_value, next_rim], axis=0)
    weights = short_weights[0]
    grad_input = (
        weights[0] * longer[:tok_rows]
        + weights[1] * longer[1 : tok_rows + 1]
        + weights[2] * longer[2:]
    )
    passed = shifted(grad_input.astype(jnp.bfloat16)[None], "pipe", -1)
    return (passed, grad_filter[None])


LANES = 128
RIM = 16
PARTS = 2
SPLIT = 4
MESH = pl.DeviceIdType.MESH


def half_step_tables(tokens, devices):
    half = tokens // 2
    odd = 2 * np.arange(half, dtype=np.int64)[:, None] + 1
    turns = (odd * np.arange(tokens, dtype=np.int64)[None, :]) % (4 * tokens)
    angles = turns * (2.0 * np.pi / (4 * tokens))
    part = half // PARTS
    share = tokens // devices // 2
    forward, inverse = [], []
    for parity in range(2):
        cosines, sines = np.cos(angles[:, parity::2]), np.sin(angles[:, parity::2])
        for first in range(0, half, part):
            forward.append(pair(np.concatenate([cosines[first : first + part], sines[first : first + part]])))
        back = np.concatenate([cosines, sines]).T
        back = np.concatenate([back, np.zeros((RIM, 2 * half))])
        for first in range(0, half, share):
            inverse.append(pair(back[first : first + share + RIM]))
    return (
        np.stack(forward).reshape(2, PARTS, 4 * part, half),
        np.stack(inverse).reshape(2, devices, 2 * (share + RIM), 2 * half),
    )


def pair(table):
    high = table.astype(jnp.bfloat16)
    low = (table - high.astype(np.float64)).astype(jnp.bfloat16)
    return np.concatenate([high, low])


def relay_kernel(
    devices, go_hbm, vb_hbm, kg_hbm, qg_hbm, sw, lf, fwd_hbm, inv_hbm,
    passed, fold_out,
    go, vb, kg, qg,
    conv_src, gated_src, both_all, gated_all, fwd, inv, mixed, woven,
    spec_both, spec_gated, packed, back_src, fold_src, back_got, fold_got, key_got, weight_got,
    load_sem, own_sem, send_sem, recv_sem, back_send, back_recv, side_send, side_recv,
):
    rows = go.shape[0]
    tokens = rows * devices
    half = tokens // 2
    share = rows // 2
    pipe = lax.axis_index("pipe")
    me = lax.axis_index("seq")
    other = 1 - pipe
    far_first = sorted(range(1, devices), key=lambda d: (abs(2 * d - devices), d))

    def gate(left, right, target):
        for block in range(devices):
            columns = pl.ds(block * LANES, LANES)
            value = left[:, columns].astype(jnp.float32) * right[:, columns].astype(jnp.float32)
            target[:, columns] = value.astype(jnp.bfloat16)

    def peer(distance):
        return lax.rem(me + distance, devices)

    def behind(distance):
        return lax.rem(me + devices - distance, devices)

    barrier = pltpu.get_barrier_semaphore()
    for distance in range(devices):
        if distance:
            pl.semaphore_signal(
                barrier, inc=1, device_id={"pipe": pipe, "seq": peer(distance)}, device_id_type=MESH
            )
        pl.semaphore_signal(
            barrier, inc=1, device_id={"pipe": other, "seq": peer(distance)}, device_id_type=MESH
        )
    loads = []
    for i, (source, target) in enumerate(
        ((go_hbm.at[0], go), (qg_hbm.at[0], qg), (kg_hbm.at[0], kg), (vb_hbm.at[0], vb), (fwd_hbm, fwd), (inv_hbm, inv))
    ):
        copy = pltpu.make_async_copy(source, target, load_sem.at[i])
        loads.append(copy)
    for copy in loads[:4]:
        copy.start()
    pl.semaphore_wait(barrier, 2 * devices - 1)

    def lanes_of(device):
        return pl.ds(pl.multiple_of(device * LANES, LANES), LANES)

    def rows_of(device):
        return pl.ds(pl.multiple_of(device * rows, rows), rows)

    first, second = pl.ds(0, LANES), pl.ds(LANES, LANES)

    def scatter(kind, pick, target):
        copies = []
        for distance in far_first:
            copy = pltpu.make_async_remote_copy(
                src_ref=pick(peer(distance)),
                dst_ref=target.at[rows_of(me)],
                send_sem=send_sem.at[kind, distance],
                recv_sem=recv_sem.at[kind, distance],
                device_id={"pipe": pipe, "seq": peer(distance)},
                device_id_type=MESH,
            )
            copy.start()
            copies.append(copy)
        own = pltpu.make_async_copy(
            pick(me), target.at[rows_of(me)], own_sem.at[kind]
        )
        own.start()
        return own, copies

    def landed(group):
        own, copies = group
        own.wait()
        for copy in copies:
            copy.wait_recv()

    filt_group = scatter(0, lambda device: lf.at[0, :, lanes_of(device)], both_all.at[0])
    loads[0].wait()
    loads[1].wait()
    gate(qg, go, conv_src)
    conv_group = scatter(1, lambda device: conv_src.at[:, lanes_of(device)], both_all.at[1])
    for copy in loads[4:]:
        copy.start()
    loads[2].wait()
    loads[3].wait()
    gate(kg, vb, gated_src)
    side = []
    for i, (source, target, at) in enumerate(
        (
            (kg, key_got.at[pl.ds(0, rows)], me),
            (kg.at[pl.ds(0, RIM)], key_got.at[pl.ds(rows, RIM)], behind(1)),
            (sw, weight_got, me),
        )
    ):
        copy = pltpu.make_async_remote_copy(
            src_ref=source, dst_ref=target, send_sem=side_send.at[i], recv_sem=side_recv.at[i],
            device_id={"pipe": other, "seq": at}, device_id_type=MESH,
        )
        copy.start()
        side.append(copy)

    gated_group = scatter(2, lambda device: gated_src.at[:, lanes_of(device)], gated_all.at[0])
    part = half // PARTS

    def transform(signal, target):
        evens, odds = [], []
        for at in range(signal.shape[0]):
            mixed[...] = signal[at].astype(jnp.float32)
            evens.append(mixed[pl.ds(0, half, stride=2), :].astype(jnp.bfloat16))
            odds.append(mixed[pl.ds(1, half, stride=2), :].astype(jnp.bfloat16))
        evens, odds = jnp.concatenate(evens, axis=1), jnp.concatenate(odds, axis=1)
        for i in range(PARTS):
            even = jnp.dot(fwd[0, i], evens, preferred_element_type=jnp.float32)
            even = even[: 2 * part] + even[2 * part :]
            odd = jnp.dot(fwd[1, i], odds, preferred_element_type=jnp.float32)
            odd = odd[: 2 * part] + odd[2 * part :]
            at = pl.ds(i * part, part)
            target[0, at, :] = even[:part] + odd[:part]
            target[1, at, :] = even[:part] - odd[:part]
            target[2, at, :] = odd[part:] + even[part:]
            target[3, at, :] = odd[part:] - even[part:]

    def pack(kind, parity, at, value):
        high = value.astype(jnp.bfloat16)
        packed[kind, parity, at, first] = high
        packed[kind, parity, at, second] = (value - high.astype(jnp.float32)).astype(jnp.bfloat16)

    def multiply(kind, spec_other):
        chunk = 64

        @pl.loop(0, half // chunk)
        def _(step):
            at = pl.ds(pl.multiple_of(step * chunk, chunk), chunk)
            low = pl.ds(pl.multiple_of(half + step * chunk, chunk), chunk)
            scale = 1.0 / tokens
            alike, cross = [], []
            for mirror in range(2):
                conv_cos = spec_both[mirror, at, second] * scale
                conv_sin = spec_both[2 + mirror, at, second] * scale
                other_cos, other_sin = spec_other[mirror, at, first], spec_other[2 + mirror, at, first]
                alike.append(conv_cos * other_cos + conv_sin * other_sin)
                cross.append(conv_sin * other_cos - conv_cos * other_sin)
            pack(kind, 0, at, alike[0] + alike[1])
            pack(kind, 0, low, cross[0] - cross[1])
            pack(kind, 1, at, alike[0] - alike[1])
            pack(kind, 1, low, cross[0] + cross[1])

    def invert(kind, block):
        for parity in range(2):
            wide = jnp.dot(inv[parity, block], packed[kind, parity], preferred_element_type=jnp.float32)
            wide = wide[: share + RIM] + wide[share + RIM :]
            wide = wide[:, :LANES] + wide[:, LANES:]
            woven[pl.ds(parity, share + RIM, stride=2), :] = wide

    def send_back(distance):
        invert(0, peer(distance))
        back_src[distance] = woven[pl.ds(0, rows + RIM), :].astype(jnp.bfloat16)
        copy = pltpu.make_async_remote_copy(
            src_ref=back_src.at[distance],
            dst_ref=back_got.at[me],
            send_sem=back_send.at[distance],
            recv_sem=back_recv.at[distance],
            device_id={"pipe": other, "seq": peer(distance)},
            device_id_type=MESH,
        )
        copy.start()
        return copy

    def send_fold(distance):
        invert(1, peer(distance))
        fold_src[distance] = woven[pl.ds(0, rows), :].astype(jnp.bfloat16)
        copy = pltpu.make_async_remote_copy(
            src_ref=fold_src.at[distance],
            dst_ref=fold_got.at[me],
            send_sem=send_sem.at[3, distance],
            recv_sem=recv_sem.at[3, distance],
            device_id={"pipe": pipe, "seq": peer(distance)},
            device_id_type=MESH,
        )
        copy.start()
        return copy

    loads[4].wait()
    landed(filt_group)
    landed(conv_group)
    transform(both_all, spec_both)
    multiply(0, spec_both)
    loads[5].wait()
    backs = [send_back(distance) for distance in far_first]
    landed(gated_group)
    transform(gated_all, spec_gated)
    multiply(1, spec_gated)
    folds = [send_fold(distance) for distance in far_first]
    backs.append(send_back(0))
    invert(1, me)
    fold_out[0, :, lanes_of(me)] = woven[pl.ds(0, rows), :]

    for copy in side:
        copy.wait_recv()
    for copy, distance in zip(backs, far_first + [0]):
        copy.wait_recv()
        columns = lanes_of(behind(distance))
        value = key_got[:, columns].astype(jnp.float32) * back_got[behind(distance)].astype(jnp.float32)
        extent = rows + RIM
        total = weight_got[0, :, columns] * value
        total += weight_got[1, :, columns] * pltpu.roll(value, extent - 1, 0)
        total += weight_got[2, :, columns] * pltpu.roll(value, extent - 2, 0)
        passed[0, :, columns] = total[:rows].astype(jnp.bfloat16)
    for copy, distance in zip(folds, far_first):
        copy.wait_recv()
        fold_out[0, :, lanes_of(behind(distance))] = fold_got[behind(distance)].astype(jnp.float32)
    for copy in filt_group[1] + conv_group[1] + gated_group[1] + side + backs + folds:
        copy.wait_send()


def relay_body(grad_out, value_branch, key_gate, query_gate, short_weights, long_filters):
    _, rows, columns = grad_out.shape
    devices = lax.axis_size("seq")
    tokens = rows * devices
    tables = [jnp.asarray(table) for table in half_step_tables(tokens, devices)]
    vmem = pl.BlockSpec(memory_space=pltpu.VMEM)
    anywhere = pl.BlockSpec(memory_space=pltpu.HBM)
    half, full = jnp.bfloat16, jnp.float32
    passed, fold = pl.pallas_call(
        functools.partial(relay_kernel, devices),
        out_shape=(
            pltpu.VMEM((1, rows, columns), half),
            pltpu.VMEM((1, rows, columns), full),
        ),
        in_specs=[anywhere] * 8,
        out_specs=(vmem, vmem),
        scratch_shapes=[pltpu.VMEM((rows, columns), half)] * 6
        + [
            pltpu.VMEM((2, tokens, LANES), half),
            pltpu.VMEM((1, tokens, LANES), half),
            pltpu.VMEM(tables[0].shape, half),
            pltpu.VMEM(tables[1].shape, half),
            pltpu.VMEM((tokens, LANES), full),
            pltpu.VMEM((rows + 2 * RIM, LANES), full),
            pltpu.VMEM((4, tokens // 2, 2 * LANES), full),
            pltpu.VMEM((4, tokens // 2, LANES), full),
            pltpu.VMEM((2, 2, tokens, 2 * LANES), half),
            pltpu.VMEM((devices, rows + RIM, LANES), half),
            pltpu.VMEM((devices, rows, LANES), half),
            pltpu.VMEM((devices, rows + RIM, LANES), half),
            pltpu.VMEM((devices, rows, LANES), half),
            pltpu.VMEM((rows + RIM, columns), half),
            pltpu.VMEM((3, 1, columns), full),
            pltpu.SemaphoreType.DMA((6,)),
            pltpu.SemaphoreType.DMA((3,)),
            pltpu.SemaphoreType.DMA((4, devices)),
            pltpu.SemaphoreType.DMA((4, devices)),
            pltpu.SemaphoreType.DMA((devices,)),
            pltpu.SemaphoreType.DMA((devices,)),
            pltpu.SemaphoreType.DMA((3,)),
            pltpu.SemaphoreType.DMA((3,)),
        ],
        compiler_params=pltpu.CompilerParams(
            collective_id=0, has_side_effects=True, vmem_limit_bytes=62 * 2**20
        ),
        cost_estimate=pl.CostEstimate(
            flops=16 * tokens * tokens * LANES, bytes_accessed=10 * tokens * tokens, transcendentals=0
        ),
    )(
        grad_out, value_branch, key_gate, query_gate,
        jnp.transpose(short_weights, (1, 0, 2)), long_filters, *tables,
    )
    return pl.pallas_call(
        settle_kernel,
        out_shape=(
            jax.ShapeDtypeStruct(passed.shape, half),
            jax.ShapeDtypeStruct(fold.shape, full),
        ),
        in_specs=[vmem, vmem],
        out_specs=(anywhere, anywhere),
        scratch_shapes=[pltpu.SemaphoreType.DMA((2, SPLIT))],
        compiler_params=pltpu.CompilerParams(vmem_limit_bytes=16 * 2**20),
    )(passed, fold)


def settle_kernel(passed, fold, passed_out, fold_out, sem):
    copies = []
    for i, (source, target) in enumerate(((fold, fold_out), (passed, passed_out))):
        step = source.shape[1] // SPLIT
        for j in range(SPLIT):
            at = pl.ds(j * step, step)
            copies.append(pltpu.make_async_copy(source.at[:, at], target.at[:, at], sem.at[i, j]))
    for copy in copies:
        copy.start()
    for copy in copies:
        copy.wait()


def solution(mesh):
    placed = (
        P("pipe", "seq", "chan"),
        P("pipe", "seq", "chan"),
        P("pipe", "seq", "chan"),
        P("pipe", "seq", "chan"),
        P("pipe", None, "chan"),
        P("pipe", "seq", "chan"),
    )

    def run(*arrays):
        _, tokens, channels = arrays[0].shape
        devices = mesh.shape["seq"]
        fits = (
            mesh.shape["pipe"] == 2
            and devices > 1
            and channels == mesh.shape["chan"] * devices * LANES
            and tokens <= 1024
            and tokens % (2 * devices * RIM) == 0
            and tokens % (2 * LANES) == 0
        )
        return jax.shard_map(
            relay_body if fits else spread_body,
            mesh=mesh,
            in_specs=placed,
            out_specs=(P("pipe", "seq", "chan"), P("pipe", "seq", "chan")),
            check_vma=False,
        )(*arrays)

    return run
```
